32 devices in a mesh: band: 4 (over x, core), pw: 8 (over z, y).
Axes of the slice: x: 2, y: 2, z: 4, core: 2. Of those that a mesh axis runs over, the one named last changes fastest.
Arguments:
- band_coeffs: bfloat16 [4, 2, 1024, 256], P('band', None, 'pw'), may hold values from -6 to 6
- potential: bfloat16 [8, 512, 512], P('pw'), may hold values from -6 to 6
- stick_list: int32 [1024, 2], replicated, may hold values from 1 to 255, as said below
Outputs:
- applied: bfloat16 [4, 2, 1024, 256], P('band', None, 'pw')
- correlation: float32 [2, 4, 4], P(None, None, 'band')
The draws below stay inside these ranges and needn't reach their ends.
Inputs may be any that keep to these rules, and one draw needn't show every extreme that they name: `stick_list`: the rows are distinct box columns (x, y), each with (x - 128)^2 + (y - 128)^2 < 128^2.
All inputs are finite; a program needn't handle non-finite values.
Results may differ from the reference program's by a relative error of at most 0.019.
Values may be sent and summed in bfloat16 or wider, within the bound.
No kernel may reach another device: no remote copies, remote signals or barrier semaphores. Data moves between devices by JAX's collectives and lax.ppermute only.
A program may use at most 64 MiB of HBM per device.

```python
import math
import jax
import jax.numpy as jnp
from jax import lax

K = 256
NG = 512
BANDS = 4
STICKS = 1024
SLAB = 8


def draw_stick_list(key, part):
    shuffled = jax.random.permutation(key, K * K).astype(jnp.int32)
    row_a = shuffled // K
    row_b = shuffled % K
    middle = K // 2
    radial = (row_a - middle) * (row_a - middle) + (row_b - middle) * (row_b - middle)
    outside = (radial >= middle * middle).astype(jnp.int32)
    chosen = shuffled[jnp.argsort(outside, stable=True)][:STICKS]
    return jnp.stack([chosen // K, chosen % K], axis=1).astype(jnp.int32)


def block_levels(key, extent, shards, smallest, largest):
    gain = 1.0
    for position, parts in shards:
        heights = jax.random.uniform(jax.random.fold_in(jax.random.fold_in(key, 6), position), (parts,), jnp.float32, smallest / len(shards), largest / len(shards))
        gain = gain * jnp.repeat(jnp.exp(heights), extent[position] // parts).reshape((-1,) + (1,) * (len(extent) - 1 - position))
    return gain


def bell_draw(rng, extent, spread, limit, shards=(), held_as=jnp.bfloat16):
    result = jax.random.normal(rng, extent, jnp.float32) * spread
    if len(shards) > 0:
        result = block_levels(rng, extent, shards, -0.22, 0.18) * result
    return jnp.clip(result, min=-limit, max=limit).astype(held_as)


def setup_inputs(seed: int = 0) -> dict:
    splits = jax.random.split(jax.random.key(seed), 4)
    return {
        "band_coeffs": bell_draw(splits[0], (BANDS, 2, STICKS, K), 1.0, 6.0, ((0, 4), (2, 8))),
        "potential": bell_draw(splits[1], (SLAB, NG, NG), 1.0, 6.0, ((0, 8),)),
        "stick_list": draw_stick_list(jax.random.fold_in(splits[3], 71), 0),
    }


def phase_table(box_count, grid_count, period, sign_value, factor):
    box_index = jnp.arange(box_count, dtype=jnp.int32) - box_count // 2
    grid_index = jnp.arange(grid_count, dtype=jnp.int32)
    phase_turns = box_index[:, None] * grid_index[None, :] % period
    angles = phase_turns.astype(jnp.float32) * (2.0 * math.pi / period)
    cos_part = (jnp.cos(angles) * factor).astype(jnp.bfloat16)
    sin_part = (sign_value * jnp.sin(angles) * factor).astype(jnp.bfloat16)
    return (cos_part, sin_part)

def complex_apply(pattern, real_in, imag_in, tables):
    cos_part = tables[0].astype(jnp.float32)
    sin_part = tables[1].astype(jnp.float32)
    real_in = real_in.astype(jnp.float32)
    imag_in = imag_in.astype(jnp.float32)
    real_out = jnp.einsum(pattern, real_in, cos_part) - jnp.einsum(pattern, imag_in, sin_part)
    imag_out = jnp.einsum(pattern, real_in, sin_part) + jnp.einsum(pattern, imag_in, cos_part)
    return (real_out, imag_out)

def sphere_mask(row_a, row_b, box_edge):
    middle = box_edge // 2
    z_level = jnp.arange(box_edge, dtype=jnp.int32) - middle
    radial = (row_a - middle) * (row_a - middle) + (row_b - middle) * (row_b - middle)
    inside = radial[:, None] + z_level[None, :] * z_level[None, :] < middle * middle
    return inside.astype(jnp.bfloat16)

def plane_work(real_in, imag_in, potential, cell_codes, box_edge, grid_len):
    leading = real_in.shape[:2]
    box_real = jnp.zeros(leading + (box_edge * box_edge,), jnp.bfloat16).at[:, :, cell_codes].set(real_in)
    box_imag = jnp.zeros(leading + (box_edge * box_edge,), jnp.bfloat16).at[:, :, cell_codes].set(imag_in)
    box_real = box_real.reshape(leading + (box_edge, box_edge))
    box_imag = box_imag.reshape(leading + (box_edge, box_edge))
    inverse = phase_table(box_edge, grid_len, grid_len, 1.0, 1.0 / math.sqrt(box_edge))
    forward = phase_table(box_edge, grid_len, grid_len, -1.0, 1.0 / math.sqrt(grid_len))
    half_real, half_imag = complex_apply('bpaj,jy->bpay', box_real, box_imag, inverse)
    half_real = half_real.astype(jnp.bfloat16)
    half_imag = half_imag.astype(jnp.bfloat16)
    field_real, field_imag = complex_apply('bpay,ax->bpxy', half_real, half_imag, inverse)
    pot_field = potential.astype(jnp.float32)[None]
    prod_real = (pot_field * field_real).astype(jnp.bfloat16)
    prod_imag = (pot_field * field_imag).astype(jnp.bfloat16)
    back_real, back_imag = complex_apply('bpxy,ax->bpay', prod_real, prod_imag, forward)
    back_real = back_real.astype(jnp.bfloat16)
    back_imag = back_imag.astype(jnp.bfloat16)
    cell_real, cell_imag = complex_apply('bpay,jy->bpaj', back_real, back_imag, forward)
    cell_real = jnp.take(cell_real.reshape(leading + (box_edge * box_edge,)), cell_codes, axis=2)
    cell_imag = jnp.take(cell_imag.reshape(leading + (box_edge * box_edge,)), cell_codes, axis=2)
    return (cell_real.astype(jnp.bfloat16), cell_imag.astype(jnp.bfloat16))

def reference(band_coeffs, potential, stick_list):
    row_a = stick_list[:, 0]
    row_b = stick_list[:, 1]
    cell_codes = row_a * K + row_b
    sphere = sphere_mask(row_a, row_b, K)
    masked = band_coeffs * sphere[None, None]
    z_inverse = phase_table(K, SLAB, NG, 1.0, 1.0 / math.sqrt(K))
    z_forward = phase_table(K, SLAB, NG, -1.0, 1.0 / math.sqrt(SLAB))

    def one_band(coeffs):
        plane_real, plane_imag = complex_apply('sk,kz->zs', coeffs[0], coeffs[1], z_inverse)
        plane_real = plane_real.astype(jnp.bfloat16)[None]
        plane_imag = plane_imag.astype(jnp.bfloat16)[None]
        back_real, back_imag = plane_work(plane_real, plane_imag, potential, cell_codes, K, NG)
        out_real, out_imag = complex_apply('zs,kz->sk', back_real[0], back_imag[0], z_forward)
        sphere_f = sphere.astype(jnp.float32)
        return jnp.stack([out_real * sphere_f, out_imag * sphere_f]).astype(jnp.bfloat16)
    applied = lax.map(one_band, masked)
    left_side = masked.astype(jnp.float32)
    right_side = applied.astype(jnp.float32)
    real_part = jnp.einsum('icsk,jcsk->ij', left_side, right_side)
    imag_part = jnp.einsum('isk,jsk->ij', left_side[:, 0], right_side[:, 1]) - jnp.einsum('isk,jsk->ij', left_side[:, 1], right_side[:, 0])
    correlation = jnp.stack([real_part, imag_part]) / math.sqrt(STICKS * K)
    return (applied, correlation.astype(jnp.float32))
```

```python
import functools
import math

import jax
import jax.numpy as jnp
import numpy as np
from jax import lax
from jax.experimental import pallas as pl
from jax.experimental.pallas import tpu as pltpu
from jax.sharding import PartitionSpec as P

F32 = jnp.float32
BF16 = jnp.bfloat16


def phases(box_index, grid_index, period, factor):
    turns = box_index[:, None] * grid_index[None, :] % period
    angles = turns * (2.0 * math.pi / period)
    return np.cos(angles) * factor, np.sin(angles) * factor


def plane_tables(box_edge, grid_len):
    half = grid_len // 2
    mats = []
    for parity in range(2):
        cos, sin = phases(
            np.arange(parity, box_edge, 2) - box_edge // 2, np.arange(half), grid_len, 1.0 / math.sqrt(box_edge)
        )
        mats.append(np.block([[cos, sin], [-sin, cos]]))
    mats = np.stack(mats)
    return jnp.asarray(mats, BF16), jnp.asarray(mats.transpose(0, 2, 1), BF16)


def z_tables(box_edge, slab_len, grid_len):
    cos, sin = phases(np.arange(box_edge) - box_edge // 2, np.arange(slab_len), grid_len, 1.0)
    inverse = np.concatenate([cos.T, sin.T]) / math.sqrt(box_edge)
    forward = np.block([[cos.T, -sin.T], [sin.T, cos.T]]) / math.sqrt(slab_len)
    return jnp.asarray(inverse, BF16), jnp.asarray(forward, BF16)


def dot_nt(left, right):
    return lax.dot_general(left, right, (((1,), (1,)), ((), ())), preferred_element_type=F32)


def dot_tn(left, right):
    return lax.dot_general(left, right, (((0,), (0,)), ((), ())), preferred_element_type=F32)


def dot_nn(left, right):
    return jnp.dot(left, right, preferred_element_type=F32)


def own_sphere(sticks_ref, stick_dev, box_edge):
    middle = box_edge // 2
    start = pl.multiple_of(lax.axis_index("pw") * stick_dev, stick_dev)
    own = sticks_ref[:, pl.ds(start, stick_dev)] - middle
    own = (own * own).astype(F32)
    radial = own[0:1] + own[1:2]
    column = jnp.broadcast_to(radial, (8, stick_dev)).T[:, 0:1]
    level = lax.broadcasted_iota(jnp.int32, (1, box_edge), 1) - middle
    return column + (level * level).astype(F32) < float(middle * middle)


def head_kernel(bands, coeffs_ref, sticks_ref, table_ref, out_ref):
    _, stick_dev, box_edge = coeffs_ref.shape
    slab_len = table_ref.shape[0] // 2
    sphere = own_sphere(sticks_ref, stick_dev, box_edge)
    table = table_ref[...]
    parts = []
    for c in range(2):
        masked = jnp.where(sphere, coeffs_ref[c].astype(F32), 0.0).astype(BF16)
        parts.append(dot_nt(table, masked))
    real = parts[0][:slab_len] - parts[1][slab_len:]
    imag = parts[0][slab_len:] + parts[1][:slab_len]
    real = real.astype(BF16).astype(F32)
    imag = imag.astype(BF16).astype(F32)
    for z in range(slab_len):
        row = jnp.concatenate([real[z : z + 1], imag[z : z + 1]], axis=0)
        for b in range(bands):
            out_ref[b * slab_len + z] = row


def plane_kernel(
    bands, recv_ref, pot_ref, sticks_ref, fwd_ref, tr_ref, out_ref, hot_a, hot_b, spread, half_ref, mid_ref, cell_ref, zeds
):
    box_edge = hot_a.shape[0]
    side = box_edge // 2
    sticks = sticks_ref.shape[1]
    groups = out_ref.shape[0]
    per = sticks // groups
    grid_len = pot_ref.shape[0]
    n_half = grid_len // 2

    codes = sticks_ref[...]
    codes = (codes & 1) * side + (codes >> 1)
    band = lax.axis_index("band")
    for g in range(groups):
        cols = slice(g * per, (g + 1) * per)
        rows = lax.broadcasted_iota(jnp.int32, (box_edge, per), 0)
        in_a = rows == codes[0:1, cols]
        in_b = rows == codes[1:2, cols]
        hot_a[:, cols] = jnp.where(in_a, 1.0, 0.0).astype(BF16)
        hot_b[:, cols] = jnp.where(in_b, 1.0, 0.0).astype(BF16)
        own = recv_ref[band * groups + g]
        for c in range(2):
            placed = jnp.where(in_b, own[c : c + 1], 0.0).astype(BF16)
            for p in range(2):
                at = p * box_edge + c * side
                spread[at : at + side, cols] = placed[p * side : (p + 1) * side]
        for i in range(bands):
            zeds[i : i + 1, cols] = recv_ref[i * groups + g, 0:1].astype(BF16)
            zeds[bands + i : bands + i + 1, cols] = recv_ref[i * groups + g, 1:2].astype(BF16)

    box = dot_nt(hot_a[...], spread[...]).astype(BF16)
    even = dot_nn(box[:, :box_edge], fwd_ref[0])
    odd = dot_nn(box[:, box_edge:], fwd_ref[1])
    low = (even + odd).astype(BF16)
    high = (even - odd).astype(BF16)
    for p in range(2):
        rows = slice(p * side, (p + 1) * side)
        for c in range(2):
            cols = slice(c * n_half, (c + 1) * n_half)
            half_ref[p, c * side : (c + 1) * side, :n_half] = low[rows, cols]
            half_ref[p, c * side : (c + 1) * side, n_half:] = high[rows, cols]

    step = 128
    for x0 in range(0, n_half, step):
        sums = {}
        for c in range(2):
            rows = slice(c * n_half + x0, c * n_half + x0 + step)
            even = dot_nn(tr_ref[0, rows], half_ref[0])
            odd = dot_nn(tr_ref[1, rows], half_ref[1])
            near = (even + odd) * pot_ref[x0 : x0 + step].astype(F32)
            far = (even - odd) * pot_ref[n_half + x0 : n_half + x0 + step].astype(F32)
            for p, both in ((0, near + far), (1, near - far)):
                sums[p, 0, c] = (both[:, :n_half] + both[:, n_half:]).astype(BF16)
                sums[p, 1, c] = (both[:, :n_half] - both[:, n_half:]).astype(BF16)
        for p in range(2):
            for q in range(2):
                left = jnp.concatenate([sums[p, q, 0], sums[p, q, 1]], axis=1)
                mid = dot_nn(left, tr_ref[q]).astype(BF16)
                for c in range(2):
                    mid_ref[p, c * n_half + x0 : c * n_half + x0 + step, q * side : (q + 1) * side] = mid[
                        :, c * side : (c + 1) * side
                    ]

    for p in range(2):
        cell = dot_nn(fwd_ref[p], mid_ref[p]) * (float(box_edge) / float(grid_len))
        cell_ref[p * box_edge : (p + 1) * box_edge] = cell.astype(BF16)

    wide = 256
    total = None
    for s0 in range(0, sticks, wide):
        cols = slice(s0, s0 + wide)
        picked = dot_nn(cell_ref[...], hot_b[:, cols])
        backs = []
        for c in range(2):
            value = None
            for p in range(2):
                at = p * box_edge + c * side
                term = jnp.sum(
                    picked[at : at + side] * hot_a[p * side : (p + 1) * side, cols].astype(F32), axis=0, keepdims=True
                )
                value = term if value is None else value + term
            backs.append(value)
        back = jnp.concatenate(backs, axis=0).astype(BF16)
        term = dot_nt(back, zeds[:, cols])
        total = term if total is None else total + term
        back = back.astype(F32)
        for g in range(s0 // per, (s0 + wide) // per):
            out_ref[g, 0:2] = back[:, g * per - s0 : (g + 1) * per - s0]
    for g in range(groups):
        out_ref[g, 2:4, : 2 * bands] = total
        out_ref[g, 2:4, 2 * bands :] = jnp.zeros((2, per - 2 * bands), F32)


def tail_kernel(bands, scale, recv_ref, sticks_ref, table_ref, out_ref, corr_ref):
    groups, _, stick_dev = recv_ref.shape
    box_edge = out_ref.shape[2]
    sphere = own_sphere(sticks_ref, stick_dev, box_edge)
    back = jnp.concatenate([recv_ref[:, 0], recv_ref[:, 1]], axis=0).astype(BF16)
    values = dot_tn(back, table_ref[...])
    for c in range(2):
        out_ref[c] = jnp.where(sphere, values[:, c * box_edge : (c + 1) * box_edge], 0.0).astype(BF16)
    total = recv_ref[0, 2:4]
    for g in range(1, groups):
        total = total + recv_ref[g, 2:4]
    real_row = total[0:1] * scale
    imag_row = total[1:2] * scale
    corr_ref[0] = real_row[:, :bands] + imag_row[:, bands : 2 * bands]
    corr_ref[1] = imag_row[:, :bands] - real_row[:, bands : 2 * bands]


def local(band_coeffs, potential, stick_list):
    groups = lax.axis_size("pw")
    bands = lax.axis_size("band") * band_coeffs.shape[0]
    _, _, stick_dev, box_edge = band_coeffs.shape
    grid_len = potential.shape[1]
    slab_len = potential.shape[0] * groups
    sticks = stick_list.shape[0]
    columns = stick_list.T
    fwd, transposed = plane_tables(box_edge, grid_len)
    z_inverse, z_forward = z_tables(box_edge, slab_len, grid_len)

    send = pl.pallas_call(
        functools.partial(head_kernel, bands),
        out_shape=jax.ShapeDtypeStruct((bands * groups, 2, stick_dev), F32),
        compiler_params=pltpu.CompilerParams(vmem_limit_bytes=4 << 20),
        name="head",
    )(band_coeffs[0], columns, z_inverse)
    planes = lax.all_to_all(send, ("band", "pw"), split_axis=0, concat_axis=0, tiled=True)
    backs = pl.pallas_call(
        functools.partial(plane_kernel, bands),
        out_shape=jax.ShapeDtypeStruct((groups, 4, stick_dev), F32),
        scratch_shapes=[
            pltpu.VMEM((box_edge, sticks), BF16),
            pltpu.VMEM((box_edge, sticks), BF16),
            pltpu.VMEM((2 * box_edge, sticks), BF16),
            pltpu.VMEM((2, box_edge, grid_len), BF16),
            pltpu.VMEM((2, grid_len, box_edge), BF16),
            pltpu.VMEM((2 * box_edge, box_edge), BF16),
            pltpu.VMEM((2 * bands, sticks), BF16),
        ],
        compiler_params=pltpu.CompilerParams(vmem_limit_bytes=32 << 20),
        name="plane",
    )(planes, potential[0], columns, fwd, transposed)
    back = lax.all_to_all(backs, "pw", split_axis=0, concat_axis=0, tiled=True)
    applied, correlation = pl.pallas_call(
        functools.partial(tail_kernel, bands, 1.0 / math.sqrt(slab_len * sticks)),
        out_shape=[
            jax.ShapeDtypeStruct((2, stick_dev, box_edge), BF16),
            jax.ShapeDtypeStruct((2, 1, bands), F32),
        ],
        compiler_params=pltpu.CompilerParams(vmem_limit_bytes=4 << 20),
        name="tail",
    )(back, columns, z_forward)
    return applied[None], correlation.transpose(0, 2, 1)


def solution(mesh):
    return jax.shard_map(
        local,
        mesh=mesh,
        in_specs=(P("band", None, "pw", None), P("pw", None, None), P()),
        out_specs=(P("band", None, "pw", None), P(None, None, "band")),
        check_vma=False,
    )
```

```python
import functools
import math

import jax
import jax.numpy as jnp
import numpy as np
from jax import lax
from jax.experimental import pallas as pl
from jax.experimental.pallas import tpu as pltpu
from jax.sharding import PartitionSpec as P

F32 = jnp.float32
BF16 = jnp.bfloat16


def phases(box_index, grid_index, period, factor):
    turns = box_index[:, None] * grid_index[None, :] % period
    angles = turns * (2.0 * math.pi / period)
    return np.cos(angles) * factor, np.sin(angles) * factor


def plane_tables(box_edge, grid_len):
    half = grid_len // 2
    mats = []
    for parity in range(2):
        cos, sin = phases(
            np.arange(parity, box_edge, 2) - box_edge // 2, np.arange(half), grid_len, 1.0 / math.sqrt(box_edge)
        )
        mats.append(np.block([[cos, sin], [-sin, cos]]))
    mats = np.stack(mats)
    return jnp.asarray(mats, BF16), jnp.asarray(mats.transpose(0, 2, 1), BF16)


def z_tables(box_edge, slab_len, grid_len):
    cos, sin = phases(np.arange(box_edge) - box_edge // 2, np.arange(slab_len), grid_len, 1.0)
    inverse = np.concatenate([cos.T, sin.T]) / math.sqrt(box_edge)
    forward = np.block([[cos.T, -sin.T], [sin.T, cos.T]]) / math.sqrt(slab_len)
    return jnp.asarray(inverse, BF16), jnp.asarray(forward, BF16)


def dot_nt(left, right):
    return lax.dot_general(left, right, (((1,), (1,)), ((), ())), preferred_element_type=F32)


def dot_tn(left, right):
    return lax.dot_general(left, right, (((0,), (0,)), ((), ())), preferred_element_type=F32)


def dot_nn(left, right):
    return jnp.dot(left, right, preferred_element_type=F32)


def own_sphere(sticks_ref, stick_dev, box_edge):
    middle = box_edge // 2
    start = pl.multiple_of(lax.axis_index("pw") * stick_dev, stick_dev)
    own = sticks_ref[:, pl.ds(start, stick_dev)] - middle
    own = (own * own).astype(F32)
    radial = own[0:1] + own[1:2]
    column = jnp.broadcast_to(radial, (8, stick_dev)).T[:, 0:1]
    level = lax.broadcasted_iota(jnp.int32, (1, box_edge), 1) - middle
    return column + (level * level).astype(F32) < float(middle * middle)


def head_kernel(bands, coeffs_hbm, sticks_hbm, table_hbm, out_ref, coeffs_ref, sticks_ref, table_ref, sems):
    copies = [
        pltpu.make_async_copy(sticks_hbm, sticks_ref, sems.at[0]),
        pltpu.make_async_copy(coeffs_hbm, coeffs_ref, sems.at[1]),
        pltpu.make_async_copy(table_hbm, table_ref, sems.at[2]),
    ]
    for copy in copies:
        copy.start()
    _, stick_dev, box_edge = coeffs_ref.shape
    copies[0].wait()
    slab_len = table_ref.shape[0] // 2
    sphere = own_sphere(sticks_ref, stick_dev, box_edge)
    copies[1].wait()
    copies[2].wait()
    table = table_ref[...]
    parts = []
    for c in range(2):
        masked = jnp.where(sphere, coeffs_ref[c].astype(F32), 0.0).astype(BF16)
        parts.append(dot_nt(table, masked))
    real = parts[0][:slab_len] - parts[1][slab_len:]
    imag = parts[0][slab_len:] + parts[1][:slab_len]
    real = real.astype(BF16).astype(F32)
    imag = imag.astype(BF16).astype(F32)
    for z in range(slab_len):
        row = jnp.concatenate([real[z : z + 1], imag[z : z + 1]], axis=0)
        for b in range(bands):
            out_ref[b * slab_len + z] = row


def plane_kernel(
    bands,
    recv_ref,
    sticks_ref,
    pot_hbm,
    fwd_hbm,
    tr_hbm,
    out_ref,
    pot_ref,
    fwd_ref,
    tr_ref,
    hot_a,
    hot_b,
    spread,
    half_ref,
    mid_ref,
    cell_ref,
    zeds,
    sems,
):
    copies = [
        pltpu.make_async_copy(fwd_hbm, fwd_ref, sems.at[0]),
        pltpu.make_async_copy(tr_hbm, tr_ref, sems.at[1]),
        pltpu.make_async_copy(pot_hbm, pot_ref, sems.at[2]),
    ]
    for copy in copies:
        copy.start()
    box_edge = hot_a.shape[0]
    side = box_edge // 2
    sticks = sticks_ref.shape[1]
    groups = out_ref.shape[0]
    per = sticks // groups
    grid_len = pot_ref.shape[0]
    n_half = grid_len // 2

    codes = sticks_ref[...]
    codes = (codes & 1) * side + (codes >> 1)
    band = lax.axis_index("band")
    for g in range(groups):
        cols = slice(g * per, (g + 1) * per)
        rows = lax.broadcasted_iota(jnp.int32, (box_edge, per), 0)
        in_a = rows == codes[0:1, cols]
        in_b = rows == codes[1:2, cols]
        hot_a[:, cols] = jnp.where(in_a, 1.0, 0.0).astype(BF16)
        hot_b[:, cols] = jnp.where(in_b, 1.0, 0.0).astype(BF16)
        own = recv_ref[band * groups + g]
        for c in range(2):
            placed = jnp.where(in_b, own[c : c + 1], 0.0).astype(BF16)
            for p in range(2):
                at = p * box_edge + c * side
                spread[at : at + side, cols] = placed[p * side : (p + 1) * side]
        for i in range(bands):
            zeds[i : i + 1, cols] = recv_ref[i * groups + g, 0:1].astype(BF16)
            zeds[bands + i : bands + i + 1, cols] = recv_ref[i * groups + g, 1:2].astype(BF16)

    box = dot_nt(hot_a[...], spread[...]).astype(BF16)
    copies[0].wait()
    even = dot_nn(box[:, :box_edge], fwd_ref[0])
    odd = dot_nn(box[:, box_edge:], fwd_ref[1])
    low = (even + odd).astype(BF16)
    high = (even - odd).astype(BF16)
    for p in range(2):
        rows = slice(p * side, (p + 1) * side)
        for c in range(2):
            cols = slice(c * n_half, (c + 1) * n_half)
            half_ref[p, c * side : (c + 1) * side, :n_half] = low[rows, cols]
            half_ref[p, c * side : (c + 1) * side, n_half:] = high[rows, cols]

    copies[1].wait()
    copies[2].wait()
    step = 128
    for x0 in range(0, n_half, step):
        sums = {}
        for c in range(2):
            rows = slice(c * n_half + x0, c * n_half + x0 + step)
            even = dot_nn(tr_ref[0, rows], half_ref[0])
            odd = dot_nn(tr_ref[1, rows], half_ref[1])
            near = (even + odd) * pot_ref[x0 : x0 + step].astype(F32)
            far = (even - odd) * pot_ref[n_half + x0 : n_half + x0 + step].astype(F32)
            for p, both in ((0, near + far), (1, near - far)):
                sums[p, 0, c] = (both[:, :n_half] + both[:, n_half:]).astype(BF16)
                sums[p, 1, c] = (both[:, :n_half] - both[:, n_half:]).astype(BF16)
        for p in range(2):
            for q in range(2):
                left = jnp.concatenate([sums[p, q, 0], sums[p, q, 1]], axis=1)
                mid = dot_nn(left, tr_ref[q]).astype(BF16)
                for c in range(2):
                    mid_ref[p, c * n_half + x0 : c * n_half + x0 + step, q * side : (q + 1) * side] = mid[
                        :, c * side : (c + 1) * side
                    ]

    for p in range(2):
        cell = dot_nn(fwd_ref[p], mid_ref[p]) * (float(box_edge) / float(grid_len))
        cell_ref[p * box_edge : (p + 1) * box_edge] = cell.astype(BF16)

    wide = 256
    total = None
    for s0 in range(0, sticks, wide):
        cols = slice(s0, s0 + wide)
        picked = dot_nn(cell_ref[...], hot_b[:, cols])
        backs = []
        for c in range(2):
            value = None
            for p in range(2):
                at = p * box_edge + c * side
                term = jnp.sum(
                    picked[at : at + side] * hot_a[p * side : (p + 1) * side, cols].astype(F32), axis=0, keepdims=True
                )
                value = term if value is None else value + term
            backs.append(value)
        back = jnp.concatenate(backs, axis=0).astype(BF16)
        term = dot_nt(back, zeds[:, cols])
        total = term if total is None else total + term
        back = back.astype(F32)
        for g in range(s0 // per, (s0 + wide) // per):
            out_ref[g, 0:2] = back[:, g * per - s0 : (g + 1) * per - s0]
    for g in range(groups):
        out_ref[g, 2:4, : 2 * bands] = total
        out_ref[g, 2:4, 2 * bands :] = jnp.zeros((2, per - 2 * bands), F32)


def tail_kernel(bands, scale, recv_ref, sticks_ref, table_ref, out_ref, corr_ref):
    groups, _, stick_dev = recv_ref.shape
    box_edge = out_ref.shape[2]
    sphere = own_sphere(sticks_ref, stick_dev, box_edge)
    back = jnp.concatenate([recv_ref[:, 0], recv_ref[:, 1]], axis=0).astype(BF16)
    values = dot_tn(back, table_ref[...])
    for c in range(2):
        out_ref[c] = jnp.where(sphere, values[:, c * box_edge : (c + 1) * box_edge], 0.0).astype(BF16)
    total = recv_ref[0, 2:4]
    for g in range(1, groups):
        total = total + recv_ref[g, 2:4]
    real_row = total[0:1] * scale
    imag_row = total[1:2] * scale
    corr_ref[0] = real_row[:, :bands] + imag_row[:, bands : 2 * bands]
    corr_ref[1] = imag_row[:, :bands] - real_row[:, bands : 2 * bands]


def local(band_coeffs, potential, stick_list):
    groups = lax.axis_size("pw")
    bands = lax.axis_size("band") * band_coeffs.shape[0]
    _, _, stick_dev, box_edge = band_coeffs.shape
    grid_len = potential.shape[1]
    slab_len = potential.shape[0] * groups
    sticks = stick_list.shape[0]
    columns = stick_list.T
    fwd, transposed = plane_tables(box_edge, grid_len)
    z_inverse, z_forward = z_tables(box_edge, slab_len, grid_len)
    in_hbm = functools.partial(pltpu.with_memory_space_constraint, memory_space=pltpu.HBM)

    send = pl.pallas_call(
        functools.partial(head_kernel, bands),
        out_shape=jax.ShapeDtypeStruct((bands * groups, 2, stick_dev), F32),
        in_specs=[pl.BlockSpec(memory_space=pltpu.HBM)] * 3,
        scratch_shapes=[
            pltpu.VMEM((2, stick_dev, box_edge), BF16),
            pltpu.VMEM((2, sticks), jnp.int32),
            pltpu.VMEM(z_inverse.shape, BF16),
            pltpu.SemaphoreType.DMA((3,)),
        ],
        compiler_params=pltpu.CompilerParams(vmem_limit_bytes=4 << 20),
        name="head",
    )(in_hbm(band_coeffs[0]), in_hbm(columns), in_hbm(z_inverse))
    planes = lax.all_to_all(send, ("band", "pw"), split_axis=0, concat_axis=0, tiled=True)
    backs = pl.pallas_call(
        functools.partial(plane_kernel, bands),
        out_shape=jax.ShapeDtypeStruct((groups, 4, stick_dev), F32),
        in_specs=[pl.BlockSpec(memory_space=pltpu.VMEM)] * 2 + [pl.BlockSpec(memory_space=pltpu.HBM)] * 3,
        scratch_shapes=[
            pltpu.VMEM((grid_len, grid_len), BF16),
            pltpu.VMEM(fwd.shape, BF16),
            pltpu.VMEM(transposed.shape, BF16),
            pltpu.VMEM((box_edge, sticks), BF16),
            pltpu.VMEM((box_edge, sticks), BF16),
            pltpu.VMEM((2 * box_edge, sticks), BF16),
            pltpu.VMEM((2, box_edge, grid_len), BF16),
            pltpu.VMEM((2, grid_len, box_edge), BF16),
            pltpu.VMEM((2 * box_edge, box_edge), BF16),
            pltpu.VMEM((2 * bands, sticks), BF16),
            pltpu.SemaphoreType.DMA((3,)),
        ],
        compiler_params=pltpu.CompilerParams(vmem_limit_bytes=32 << 20),
        name="plane",
    )(planes, columns, in_hbm(potential[0]), in_hbm(fwd), in_hbm(transposed))
    back = lax.all_to_all(backs, "pw", split_axis=0, concat_axis=0, tiled=True)
    applied, correlation = pl.pallas_call(
        functools.partial(tail_kernel, bands, 1.0 / math.sqrt(slab_len * sticks)),
        out_shape=[
            jax.ShapeDtypeStruct((2, stick_dev, box_edge), BF16),
            jax.ShapeDtypeStruct((2, 1, bands), F32),
        ],
        compiler_params=pltpu.CompilerParams(vmem_limit_bytes=4 << 20),
        name="tail",
    )(back, columns, z_forward)
    return applied[None], correlation.transpose(0, 2, 1)


def solution(mesh):
    return jax.shard_map(
        local,
        mesh=mesh,
        in_specs=(P("band", None, "pw", None), P("pw", None, None), P()),
        out_specs=(P("band", None, "pw", None), P(None, None, "band")),
        check_vma=False,
    )
```

```python
import functools
import math

import jax
import jax.numpy as jnp
import numpy as np
from jax import lax
from jax.experimental import pallas as pl
from jax.experimental.pallas import tpu as pltpu
from jax.sharding import PartitionSpec as P

F32 = jnp.float32
BF16 = jnp.bfloat16


def phases(box_index, grid_index, period, factor):
    turns = box_index[:, None] * grid_index[None, :] % period
    angles = turns * (2.0 * math.pi / period)
    return np.cos(angles) * factor, np.sin(angles) * factor


def plane_tables(box_edge, grid_len):
    half = grid_len // 2
    mats = []
    for parity in range(2):
        cos, sin = phases(
            np.arange(parity, box_edge, 2) - box_edge // 2, np.arange(half), grid_len, 1.0 / math.sqrt(box_edge)
        )
        mats.append(np.block([[cos, sin], [-sin, cos]]))
    mats = np.stack(mats)
    return jnp.asarray(mats, BF16), jnp.asarray(mats.transpose(0, 2, 1), BF16)


def z_tables(box_edge, slab_len, grid_len):
    cos, sin = phases(np.arange(box_edge) - box_edge // 2, np.arange(slab_len), grid_len, 1.0)
    inverse = np.concatenate([cos.T, sin.T]) / math.sqrt(box_edge)
    forward = np.block([[cos.T, -sin.T], [sin.T, cos.T]]) / math.sqrt(slab_len)
    return jnp.asarray(inverse, BF16), jnp.asarray(forward, BF16)


def dot_nt(left, right):
    return lax.dot_general(left, right, (((1,), (1,)), ((), ())), preferred_element_type=F32)


def dot_tn(left, right):
    return lax.dot_general(left, right, (((0,), (0,)), ((), ())), preferred_element_type=F32)


def dot_nn(left, right):
    return jnp.dot(left, right, preferred_element_type=F32)


def own_sphere(sticks_ref, stick_dev, box_edge):
    middle = box_edge // 2
    start = pl.multiple_of(lax.axis_index("pw") * stick_dev, stick_dev)
    own = sticks_ref[:, pl.ds(start, stick_dev)] - middle
    own = (own * own).astype(F32)
    radial = own[0:1] + own[1:2]
    column = jnp.broadcast_to(radial, (8, stick_dev)).T[:, 0:1]
    level = lax.broadcasted_iota(jnp.int32, (1, box_edge), 1) - middle
    return column + (level * level).astype(F32) < float(middle * middle)


def head_kernel(
    mates,
    coeffs_hbm,
    sticks_hbm,
    table_hbm,
    pot_hbm,
    fwd_hbm,
    tr_hbm,
    out_ref,
    hot_a,
    hot_b,
    pot_ref,
    fwd_ref,
    tr_ref,
    coeffs_ref,
    sticks_ref,
    table_ref,
    sems,
):
    pairs = [
        (sticks_hbm, sticks_ref),
        (coeffs_hbm, coeffs_ref),
        (table_hbm, table_ref),
        (fwd_hbm, fwd_ref),
        (tr_hbm, tr_ref),
        (pot_hbm, pot_ref),
    ]
    copies = [pltpu.make_async_copy(src, dst, sems.at[n]) for n, (src, dst) in enumerate(pairs)]
    for copy in copies:
        copy.start()
    _, stick_dev, box_edge = coeffs_ref.shape
    slab_len = table_ref.shape[0] // 2
    side = box_edge // 2
    copies[0].wait()
    sphere = own_sphere(sticks_ref, stick_dev, box_edge)
    copies[1].wait()
    copies[2].wait()
    table = table_ref[...]
    parts = []
    for c in range(2):
        masked = jnp.where(sphere, coeffs_ref[c].astype(F32), 0.0).astype(BF16)
        parts.append(dot_nt(table, masked))
    real = parts[0][:slab_len] - parts[1][slab_len:]
    imag = parts[0][slab_len:] + parts[1][:slab_len]
    real = real.astype(BF16).astype(F32)
    imag = imag.astype(BF16).astype(F32)
    for z in range(slab_len):
        row = jnp.concatenate([real[z : z + 1], imag[z : z + 1]], axis=0)
        for b in range(mates):
            out_ref[(slab_len - 1 - z) * mates + b] = row

    codes = sticks_ref[...]
    codes = (codes & 1) * side + (codes >> 1)
    rows = lax.broadcasted_iota(jnp.int32, (box_edge, stick_dev), 0)
    for at in range(0, codes.shape[1], stick_dev):
        cols = slice(at, at + stick_dev)
        hot_a[:, cols] = jnp.where(rows == codes[0:1, cols], 1.0, 0.0).astype(BF16)
        hot_b[:, cols] = jnp.where(rows == codes[1:2, cols], 1.0, 0.0).astype(BF16)
    for copy in copies[3:]:
        copy.wait()


def plane_kernel(
    mates, recv_ref, hot_a, hot_b, pot_ref, fwd_ref, tr_ref, cell_ref, spread, half_ref, mid_ref
):
    box_edge, sticks = hot_a.shape
    side = box_edge // 2
    groups = recv_ref.shape[0] // mates
    per = sticks // groups
    grid_len = pot_ref.shape[0]
    n_half = grid_len // 2

    own_mate = lax.rem(lax.axis_index("band"), mates)
    for g in range(groups):
        cols = slice(g * per, (g + 1) * per)
        at = (groups - 1 - g) * mates
        own = recv_ref[at + own_mate].astype(BF16)
        for c in range(2):
            placed = hot_b[:, cols] * own[c : c + 1]
            for p in range(2):
                row = p * box_edge + c * side
                spread[row : row + side, cols] = placed[p * side : (p + 1) * side]

    box = dot_nt(hot_a[...], spread[...]).astype(BF16)
    even = dot_nn(box[:, :box_edge], fwd_ref[0])
    odd = dot_nn(box[:, box_edge:], fwd_ref[1])
    low = (even + odd).astype(BF16)
    high = (even - odd).astype(BF16)
    for p in range(2):
        rows = slice(p * side, (p + 1) * side)
        for c in range(2):
            cols = slice(c * n_half, (c + 1) * n_half)
            half_ref[p, c * side : (c + 1) * side, :n_half] = low[rows, cols]
            half_ref[p, c * side : (c + 1) * side, n_half:] = high[rows, cols]

    step = 128
    for x0 in range(0, n_half, step):
        sums = {}
        for c in range(2):
            rows = slice(c * n_half + x0, c * n_half + x0 + step)
            even = dot_nn(tr_ref[0, rows], half_ref[0])
            odd = dot_nn(tr_ref[1, rows], half_ref[1])
            near = (even + odd) * pot_ref[x0 : x0 + step].astype(F32)
            far = (even - odd) * pot_ref[n_half + x0 : n_half + x0 + step].astype(F32)
            for p, both in ((0, near + far), (1, near - far)):
                sums[p, 0, c] = (both[:, :n_half] + both[:, n_half:]).astype(BF16)
                sums[p, 1, c] = (both[:, :n_half] - both[:, n_half:]).astype(BF16)
        for p in range(2):
            for q in range(2):
                left = jnp.concatenate([sums[p, q, 0], sums[p, q, 1]], axis=1)
                mid = dot_nn(left, tr_ref[q]).astype(BF16)
                for c in range(2):
                    mid_ref[p, c * n_half + x0 : c * n_half + x0 + step, q * side : (q + 1) * side] = mid[
                        :, c * side : (c + 1) * side
                    ]

    for p in range(2):
        cell = dot_nn(fwd_ref[p], mid_ref[p]) * (float(box_edge) / float(grid_len))
        cell_ref[p * box_edge : (p + 1) * box_edge] = cell.astype(BF16)


def read_kernel(mates, count, *refs):
    cell_ref, hot_a, hot_b = refs[:3]
    planes = refs[3 : 3 + count]
    out_ref, all_zeds = refs[3 + count :]
    box_edge, sticks = hot_a.shape
    side = box_edge // 2
    groups = out_ref.shape[0]
    per = sticks // groups

    backs = [[], []]
    wide = 256
    for s0 in range(0, sticks, wide):
        cols = slice(s0, s0 + wide)
        picked = dot_nn(cell_ref[...], hot_b[:, cols])
        for c in range(2):
            value = None
            for p in range(2):
                at = p * box_edge + c * side
                term = picked[at : at + side] * hot_a[p * side : (p + 1) * side, cols].astype(F32)
                value = term if value is None else value + term
            backs[c].append(jnp.sum(value, axis=0, keepdims=True))
    back = jnp.concatenate([jnp.concatenate(parts, axis=1) for parts in backs], axis=0)

    here = lax.axis_index("band") // mates
    for s in range(count):
        source = lax.rem(here - s + count, count)
        all_zeds[source, 2 * mates :] = jnp.zeros((8 - 2 * mates, sticks), F32)
        for g in range(groups):
            at = (groups - 1 - g) * mates
            both = [planes[s][at + b, c : c + 1] for c in range(2) for b in range(mates)]
            all_zeds[source, : 2 * mates, g * per : (g + 1) * per] = jnp.concatenate(both, axis=0)

    lanes = all_zeds.shape[0] * all_zeds.shape[1]
    total = dot_nt(back.astype(BF16), all_zeds[...].reshape(lanes, sticks).astype(BF16))
    back = back.astype(BF16).astype(F32)
    for g in range(groups):
        out_ref[groups - 1 - g, 0:2] = back[:, g * per : (g + 1) * per]
        out_ref[groups - 1 - g, 2:4, :lanes] = total
        out_ref[groups - 1 - g, 2:4, lanes:] = jnp.zeros((2, per - lanes), F32)


def tail_kernel(mates, scale, recv_ref, sticks_ref, table_ref, out_ref, corr_ref):
    groups, _, stick_dev = recv_ref.shape
    box_edge = out_ref.shape[2]
    sphere = own_sphere(sticks_ref, stick_dev, box_edge)
    rows = [recv_ref[groups - 1 - g, c : c + 1] for c in range(2) for g in range(groups)]
    back = jnp.concatenate(rows, axis=0).astype(BF16)
    values = dot_tn(back, table_ref[...])
    for c in range(2):
        out_ref[c] = jnp.where(sphere, values[:, c * box_edge : (c + 1) * box_edge], 0.0).astype(BF16)
    total = recv_ref[0, 2:4]
    for g in range(1, groups):
        total = total + recv_ref[g, 2:4]
    total = total * scale
    for q in range(corr_ref.shape[2] // mates):
        re, im = slice(8 * q, 8 * q + mates), slice(8 * q + mates, 8 * q + 2 * mates)
        corr_ref[0, :, q * mates : (q + 1) * mates] = total[0:1, re] + total[1:2, im]
        corr_ref[1, :, q * mates : (q + 1) * mates] = total[1:2, re] - total[0:1, im]


def local(band_coeffs, potential, stick_list):
    groups = lax.axis_size("pw")
    bands = lax.axis_size("band")
    _, _, stick_dev, box_edge = band_coeffs.shape
    grid_len = potential.shape[1]
    slab_len = potential.shape[0] * groups
    sticks = stick_list.shape[0]
    columns = stick_list.T
    fwd, transposed = plane_tables(box_edge, grid_len)
    z_inverse, z_forward = z_tables(box_edge, slab_len, grid_len)
    in_hbm = functools.partial(pltpu.with_memory_space_constraint, memory_space=pltpu.HBM)
    hbm, vmem = pl.BlockSpec(memory_space=pltpu.HBM), pl.BlockSpec(memory_space=pltpu.VMEM)
    mates = 2 if bands % 2 == 0 else 1
    count = bands // mates

    send, *operands = pl.pallas_call(
        functools.partial(head_kernel, mates),
        out_shape=[
            jax.ShapeDtypeStruct((mates * groups, 2, stick_dev), F32),
            jax.ShapeDtypeStruct((box_edge, sticks), BF16),
            jax.ShapeDtypeStruct((box_edge, sticks), BF16),
            jax.ShapeDtypeStruct((grid_len, grid_len), BF16),
            jax.ShapeDtypeStruct(fwd.shape, BF16),
            jax.ShapeDtypeStruct(transposed.shape, BF16),
        ],
        in_specs=[hbm] * 6,
        out_specs=[vmem] * 6,
        scratch_shapes=[
            pltpu.VMEM((2, stick_dev, box_edge), BF16),
            pltpu.VMEM((2, sticks), jnp.int32),
            pltpu.VMEM(z_inverse.shape, BF16),
            pltpu.SemaphoreType.DMA((6,)),
        ],
        compiler_params=pltpu.CompilerParams(vmem_limit_bytes=8 << 20),
        name="head",
    )(
        in_hbm(band_coeffs[0]),
        in_hbm(columns),
        in_hbm(z_inverse),
        in_hbm(potential[0]),
        in_hbm(fwd),
        in_hbm(transposed),
    )
    hot_a, hot_b = operands[:2]
    order = [
        [(q * mates + b) * groups + g for g in reversed(range(groups)) for b in range(mates)] for q in range(count)
    ]
    planes = lax.all_to_all(
        send, ("band", "pw"), split_axis=0, concat_axis=0, tiled=True, axis_index_groups=order
    )
    others = [
        lax.ppermute(planes, "band", [(b, (b + s * mates) % bands) for b in range(bands)]) for s in range(1, count)
    ]
    cell = pl.pallas_call(
        functools.partial(plane_kernel, mates),
        out_shape=jax.ShapeDtypeStruct((2 * box_edge, box_edge), BF16),
        in_specs=[vmem] * 6,
        out_specs=vmem,
        scratch_shapes=[
            pltpu.VMEM((2 * box_edge, sticks), BF16),
            pltpu.VMEM((2, box_edge, grid_len), BF16),
            pltpu.VMEM((2, grid_len, box_edge), BF16),
        ],
        compiler_params=pltpu.CompilerParams(vmem_limit_bytes=16 << 20),
        cost_estimate=pl.CostEstimate(flops=1_400_000_000, bytes_accessed=3 << 20, transcendentals=0),
        name="plane",
    )(planes, *operands)
    backs = pl.pallas_call(
        functools.partial(read_kernel, mates, count),
        out_shape=jax.ShapeDtypeStruct((groups, 4, stick_dev), F32),
        in_specs=[vmem] * (3 + count),
        out_specs=vmem,
        scratch_shapes=[pltpu.VMEM((count, 8, sticks), F32)],
        compiler_params=pltpu.CompilerParams(vmem_limit_bytes=16 << 20),
        name="read",
    )(cell, hot_a, hot_b, planes, *others)
    back = lax.all_to_all(
        backs,
        "pw",
        split_axis=0,
        concat_axis=0,
        tiled=True,
        axis_index_groups=[list(reversed(range(groups)))],
    )
    applied, correlation = pl.pallas_call(
        functools.partial(tail_kernel, mates, 1.0 / math.sqrt(slab_len * sticks)),
        out_shape=[
            jax.ShapeDtypeStruct((2, stick_dev, box_edge), BF16),
            jax.ShapeDtypeStruct((2, 1, bands), F32),
        ],
        compiler_params=pltpu.CompilerParams(vmem_limit_bytes=4 << 20),
        name="tail",
    )(back, columns, z_forward)
    return applied[None], correlation.transpose(0, 2, 1)


def solution(mesh):
    return jax.shard_map(
        local,
        mesh=mesh,
        in_specs=(P("band", None, "pw", None), P("pw", None, None), P()),
        out_specs=(P("band", None, "pw", None), P(None, None, "band")),
        check_vma=False,
    )
```

```python
import functools
import math

import jax
import jax.numpy as jnp
import numpy as np
from jax import lax
from jax.experimental import pallas as pl
from jax.experimental.pallas import tpu as pltpu
from jax.sharding import PartitionSpec as P

F32 = jnp.float32
BF16 = jnp.bfloat16


def led(group, mate, groups, mates):
    members = [(g, b) for g in range(groups) for b in range(mates)]
    members.remove((group, mate))
    return [(group, mate), *members]


def phases(box_index, grid_index, period, factor):
    turns = box_index[:, None] * grid_index[None, :] % period
    angles = turns * (2.0 * math.pi / period)
    return np.cos(angles) * factor, np.sin(angles) * factor


def plane_tables(box_edge, grid_len):
    half = grid_len // 2
    mats = []
    for parity in range(2):
        cos, sin = phases(
            np.arange(parity, box_edge, 2) - box_edge // 2, np.arange(half), grid_len, 1.0 / math.sqrt(box_edge)
        )
        mats.append(np.block([[cos, sin], [-sin, cos]]))
    mats = np.stack(mats)
    return jnp.asarray(mats, BF16), jnp.asarray(mats.transpose(0, 2, 1), BF16)


def z_tables(box_edge, slab_len, grid_len):
    cos, sin = phases(np.arange(box_edge) - box_edge // 2, np.arange(slab_len), grid_len, 1.0)
    inverse = np.concatenate([cos.T, sin.T]) / math.sqrt(box_edge)
    forward = np.block([[cos.T, -sin.T], [sin.T, cos.T]]) / math.sqrt(slab_len)
    return jnp.asarray(inverse, BF16), jnp.asarray(forward, BF16)


def dot_nt(left, right):
    return lax.dot_general(left, right, (((1,), (1,)), ((), ())), preferred_element_type=F32)


def dot_tn(left, right):
    return lax.dot_general(left, right, (((0,), (0,)), ((), ())), preferred_element_type=F32)


def dot_nn(left, right):
    return jnp.dot(left, right, preferred_element_type=F32)


def own_sphere(sticks_ref, stick_dev, box_edge):
    middle = box_edge // 2
    start = pl.multiple_of(lax.axis_index("pw") * stick_dev, stick_dev)
    own = sticks_ref[:, pl.ds(start, stick_dev)] - middle
    own = (own * own).astype(F32)
    radial = own[0:1] + own[1:2]
    column = jnp.broadcast_to(radial, (8, stick_dev)).T[:, 0:1]
    level = lax.broadcasted_iota(jnp.int32, (1, box_edge), 1) - middle
    return column + (level * level).astype(F32) < float(middle * middle)


def head_kernel(
    mates,
    first,
    coeffs_hbm,
    sticks_hbm,
    table_hbm,
    pot_hbm,
    fwd_hbm,
    tr_hbm,
    out_ref,
    hot_a,
    hot_b,
    pot_ref,
    fwd_ref,
    tr_ref,
    coeffs_ref,
    sticks_ref,
    table_ref,
    sems,
):
    pairs = [
        (sticks_hbm, sticks_ref),
        (coeffs_hbm, coeffs_ref),
        (table_hbm, table_ref),
        (fwd_hbm, fwd_ref),
        (tr_hbm, tr_ref),
        (pot_hbm, pot_ref),
    ]
    copies = [pltpu.make_async_copy(src, dst, sems.at[n]) for n, (src, dst) in enumerate(pairs)]
    for copy in copies:
        copy.start()
    _, stick_dev, box_edge = coeffs_ref.shape
    slab_len = table_ref.shape[0] // 2
    side = box_edge // 2
    copies[0].wait()
    sphere = own_sphere(sticks_ref, stick_dev, box_edge)
    copies[1].wait()
    copies[2].wait()
    table = table_ref[...]
    parts = []
    for c in range(2):
        masked = jnp.where(sphere, coeffs_ref[c].astype(F32), 0.0).astype(BF16)
        parts.append(dot_nt(table, masked))
    real = parts[0][:slab_len] - parts[1][slab_len:]
    imag = parts[0][slab_len:] + parts[1][:slab_len]
    real = real.astype(BF16).astype(F32)
    imag = imag.astype(BF16).astype(F32)
    for z in range(slab_len):
        row = jnp.concatenate([real[z : z + 1], imag[z : z + 1]], axis=0)
        for b in range(mates):
            out_ref[first.index((z, b))] = row

    codes = sticks_ref[...]
    codes = (codes & 1) * side + (codes >> 1)
    rows = lax.broadcasted_iota(jnp.int32, (box_edge, stick_dev), 0)
    for at in range(0, codes.shape[1], stick_dev):
        cols = slice(at, at + stick_dev)
        hot_a[:, cols] = jnp.where(rows == codes[0:1, cols], 1.0, 0.0).astype(BF16)
        hot_b[:, cols] = jnp.where(rows == codes[1:2, cols], 1.0, 0.0).astype(BF16)
    for copy in copies[3:]:
        copy.wait()


def plane_kernel(
    mates, first, recv_ref, hot_a, hot_b, pot_ref, fwd_ref, tr_ref, cell_ref, spread, half_ref, mid_ref
):
    box_edge, sticks = hot_a.shape
    side = box_edge // 2
    groups = recv_ref.shape[0] // mates
    per = sticks // groups
    grid_len = pot_ref.shape[0]
    n_half = grid_len // 2

    own_mate = lax.rem(lax.axis_index("band"), mates)
    for g in range(groups):
        cols = slice(g * per, (g + 1) * per)
        own = recv_ref[first.index((g, 0))]
        for b in range(1, mates):
            own = jnp.where(own_mate == b, recv_ref[first.index((g, b))], own)
        own = own.astype(BF16)
        for c in range(2):
            placed = hot_b[:, cols] * own[c : c + 1]
            for p in range(2):
                row = p * box_edge + c * side
                spread[row : row + side, cols] = placed[p * side : (p + 1) * side]

    box = dot_nt(hot_a[...], spread[...]).astype(BF16)
    even = dot_nn(box[:, :box_edge], fwd_ref[0])
    odd = dot_nn(box[:, box_edge:], fwd_ref[1])
    low = (even + odd).astype(BF16)
    high = (even - odd).astype(BF16)
    for p in range(2):
        rows = slice(p * side, (p + 1) * side)
        for c in range(2):
            cols = slice(c * n_half, (c + 1) * n_half)
            half_ref[p, c * side : (c + 1) * side, :n_half] = low[rows, cols]
            half_ref[p, c * side : (c + 1) * side, n_half:] = high[rows, cols]

    step = 128
    for x0 in range(0, n_half, step):
        sums = {}
        for c in range(2):
            rows = slice(c * n_half + x0, c * n_half + x0 + step)
            even = dot_nn(tr_ref[0, rows], half_ref[0])
            odd = dot_nn(tr_ref[1, rows], half_ref[1])
            near = (even + odd) * pot_ref[x0 : x0 + step].astype(F32)
            far = (even - odd) * pot_ref[n_half + x0 : n_half + x0 + step].astype(F32)
            for p, both in ((0, near + far), (1, near - far)):
                sums[p, 0, c] = (both[:, :n_half] + both[:, n_half:]).astype(BF16)
                sums[p, 1, c] = (both[:, :n_half] - both[:, n_half:]).astype(BF16)
        for p in range(2):
            for q in range(2):
                left = jnp.concatenate([sums[p, q, 0], sums[p, q, 1]], axis=1)
                mid = dot_nn(left, tr_ref[q]).astype(BF16)
                for c in range(2):
                    mid_ref[p, c * n_half + x0 : c * n_half + x0 + step, q * side : (q + 1) * side] = mid[
                        :, c * side : (c + 1) * side
                    ]

    for p in range(2):
        cell = dot_nn(fwd_ref[p], mid_ref[p]) * (float(box_edge) / float(grid_len))
        cell_ref[p * box_edge : (p + 1) * box_edge] = cell.astype(BF16)


def read_kernel(mates, count, first, second, *refs):
    cell_ref, hot_a, hot_b = refs[:3]
    planes = refs[3 : 3 + count]
    out_ref, all_zeds = refs[3 + count :]
    box_edge, sticks = hot_a.shape
    side = box_edge // 2
    groups = out_ref.shape[0] // mates
    per = sticks // groups

    backs = [[], []]
    wide = 256
    for s0 in range(0, sticks, wide):
        cols = slice(s0, s0 + wide)
        picked = dot_nn(cell_ref[...], hot_b[:, cols])
        for c in range(2):
            value = None
            for p in range(2):
                at = p * box_edge + c * side
                term = picked[at : at + side] * hot_a[p * side : (p + 1) * side, cols].astype(F32)
                value = term if value is None else value + term
            backs[c].append(jnp.sum(value, axis=0, keepdims=True))
    back = jnp.concatenate([jnp.concatenate(parts, axis=1) for parts in backs], axis=0)

    here = lax.axis_index("band") // mates
    for s in range(count):
        source = lax.rem(here - s + count, count)
        all_zeds[source, 2 * mates :] = jnp.zeros((8 - 2 * mates, sticks), F32)
        for g in range(groups):
            both = [planes[s][first.index((g, b)), c : c + 1] for c in range(2) for b in range(mates)]
            all_zeds[source, : 2 * mates, g * per : (g + 1) * per] = jnp.concatenate(both, axis=0)

    lanes = all_zeds.shape[0] * all_zeds.shape[1]
    total = dot_nt(back.astype(BF16), all_zeds[...].reshape(lanes, sticks).astype(BF16))
    back = back.astype(BF16).astype(F32)
    for g in range(groups):
        for b in range(mates):
            at = second.index((g, b))
            out_ref[at, 0:2] = back[:, g * per : (g + 1) * per]
            out_ref[at, 2:4, :lanes] = total
            out_ref[at, 2:4, lanes:] = jnp.zeros((2, per - lanes), F32)


def tail_kernel(mates, second, scale, recv_ref, sticks_ref, table_ref, out_ref, corr_ref):
    blocks, _, stick_dev = recv_ref.shape
    groups = blocks // mates
    own_mate = lax.rem(lax.axis_index("band"), mates)
    box_edge = out_ref.shape[2]
    sphere = own_sphere(sticks_ref, stick_dev, box_edge)
    picked = []
    for g in range(groups):
        own = recv_ref[second.index((g, 0))]
        for b in range(1, mates):
            own = jnp.where(own_mate == b, recv_ref[second.index((g, b))], own)
        picked.append(own)
    back = jnp.concatenate([own[c : c + 1] for c in range(2) for own in picked], axis=0).astype(BF16)
    values = dot_tn(back, table_ref[...])
    for c in range(2):
        out_ref[c] = jnp.where(sphere, values[:, c * box_edge : (c + 1) * box_edge], 0.0).astype(BF16)
    total = picked[0][2:4]
    for own in picked[1:]:
        total = total + own[2:4]
    total = total * scale
    for q in range(corr_ref.shape[2] // mates):
        re, im = slice(8 * q, 8 * q + mates), slice(8 * q + mates, 8 * q + 2 * mates)
        corr_ref[0, :, q * mates : (q + 1) * mates] = total[0:1, re] + total[1:2, im]
        corr_ref[1, :, q * mates : (q + 1) * mates] = total[1:2, re] - total[0:1, im]


def local(band_coeffs, potential, stick_list):
    groups = lax.axis_size("pw")
    bands = lax.axis_size("band")
    _, _, stick_dev, box_edge = band_coeffs.shape
    grid_len = potential.shape[1]
    slab_len = potential.shape[0] * groups
    sticks = stick_list.shape[0]
    columns = stick_list.T
    fwd, transposed = plane_tables(box_edge, grid_len)
    z_inverse, z_forward = z_tables(box_edge, slab_len, grid_len)
    in_hbm = functools.partial(pltpu.with_memory_space_constraint, memory_space=pltpu.HBM)
    hbm, vmem = pl.BlockSpec(memory_space=pltpu.HBM), pl.BlockSpec(memory_space=pltpu.VMEM)
    mates = 2 if bands % 2 == 0 else 1
    count = bands // mates
    first = led(groups - 1, 1, groups, mates)
    second = led(groups - 1, 1, groups, mates)

    send, *operands = pl.pallas_call(
        functools.partial(head_kernel, mates, first),
        out_shape=[
            jax.ShapeDtypeStruct((mates * groups, 2, stick_dev), F32),
            jax.ShapeDtypeStruct((box_edge, sticks), BF16),
            jax.ShapeDtypeStruct((box_edge, sticks), BF16),
            jax.ShapeDtypeStruct((grid_len, grid_len), BF16),
            jax.ShapeDtypeStruct(fwd.shape, BF16),
            jax.ShapeDtypeStruct(transposed.shape, BF16),
        ],
        in_specs=[hbm] * 6,
        out_specs=[vmem] * 6,
        scratch_shapes=[
            pltpu.VMEM((2, stick_dev, box_edge), BF16),
            pltpu.VMEM((2, sticks), jnp.int32),
            pltpu.VMEM(z_inverse.shape, BF16),
            pltpu.SemaphoreType.DMA((6,)),
        ],
        compiler_params=pltpu.CompilerParams(vmem_limit_bytes=8 << 20),
        name="head",
    )(
        in_hbm(band_coeffs[0]),
        in_hbm(columns),
        in_hbm(z_inverse),
        in_hbm(potential[0]),
        in_hbm(fwd),
        in_hbm(transposed),
    )
    hot_a, hot_b = operands[:2]
    order = [[(q * mates + b) * groups + g for g, b in first] for q in range(count)]
    planes = lax.all_to_all(
        send, ("band", "pw"), split_axis=0, concat_axis=0, tiled=True, axis_index_groups=order
    )
    others = [
        lax.ppermute(planes, "band", [(b, (b + s * mates) % bands) for b in range(bands)]) for s in range(1, count)
    ]
    cell = pl.pallas_call(
        functools.partial(plane_kernel, mates, first),
        out_shape=jax.ShapeDtypeStruct((2 * box_edge, box_edge), BF16),
        in_specs=[vmem] * 6,
        out_specs=vmem,
        scratch_shapes=[
            pltpu.VMEM((2 * box_edge, sticks), BF16),
            pltpu.VMEM((2, box_edge, grid_len), BF16),
            pltpu.VMEM((2, grid_len, box_edge), BF16),
        ],
        compiler_params=pltpu.CompilerParams(vmem_limit_bytes=16 << 20),
        cost_estimate=pl.CostEstimate(flops=1_400_000_000, bytes_accessed=3 << 20, transcendentals=0),
        name="plane",
    )(planes, *operands)
    backs = pl.pallas_call(
        functools.partial(read_kernel, mates, count, first, second),
        out_shape=jax.ShapeDtypeStruct((mates * groups, 4, stick_dev), F32),
        in_specs=[vmem] * (3 + count),
        out_specs=vmem,
        scratch_shapes=[pltpu.VMEM((count, 8, sticks), F32)],
        compiler_params=pltpu.CompilerParams(vmem_limit_bytes=16 << 20),
        name="read",
    )(cell, hot_a, hot_b, planes, *others)
    back = lax.all_to_all(
        backs,
        ("band", "pw"),
        split_axis=0,
        concat_axis=0,
        tiled=True,
        axis_index_groups=[[(q * mates + b) * groups + g for g, b in second] for q in range(count)],
    )
    applied, correlation = pl.pallas_call(
        functools.partial(tail_kernel, mates, second, 1.0 / math.sqrt(slab_len * sticks)),
        out_shape=[
            jax.ShapeDtypeStruct((2, stick_dev, box_edge), BF16),
            jax.ShapeDtypeStruct((2, 1, bands), F32),
        ],
        compiler_params=pltpu.CompilerParams(vmem_limit_bytes=4 << 20),
        name="tail",
    )(back, columns, z_forward)
    return applied[None], correlation.transpose(0, 2, 1)


def solution(mesh):
    return jax.shard_map(
        local,
        mesh=mesh,
        in_specs=(P("band", None, "pw", None), P("pw", None, None), P()),
        out_specs=(P("band", None, "pw", None), P(None, None, "band")),
        check_vma=False,
    )
```

```python
import functools
import math

import jax
import jax.numpy as jnp
import numpy as np
from jax import lax
from jax.experimental import pallas as pl
from jax.experimental.pallas import tpu as pltpu
from jax.sharding import PartitionSpec as P

F32 = jnp.float32
BF16 = jnp.bfloat16


def place_of(group, mate, groups, mates):
    return (groups - 1 - group) * mates + mates - 1 - mate


def phases(box_index, grid_index, period, factor):
    turns = box_index[:, None] * grid_index[None, :] % period
    angles = turns * (2.0 * math.pi / period)
    return np.cos(angles) * factor, np.sin(angles) * factor


def plane_tables(box_edge, grid_len):
    half = grid_len // 2
    mats = []
    for parity in range(2):
        cos, sin = phases(
            np.arange(parity, box_edge, 2) - box_edge // 2, np.arange(half), grid_len, 1.0 / math.sqrt(box_edge)
        )
        mats.append(np.block([[cos, sin], [-sin, cos]]))
    mats = np.stack(mats)
    return jnp.asarray(mats[:, : box_edge // 2], BF16), jnp.asarray(mats.transpose(0, 2, 1)[:, :half], BF16)


def z_tables(box_edge, slab_len, grid_len):
    cos, sin = phases(np.arange(box_edge) - box_edge // 2, np.arange(slab_len), grid_len, 1.0)
    inverse = np.stack([np.concatenate([cos.T, -sin.T], 1), np.concatenate([sin.T, cos.T], 1)], 1)
    inverse = inverse.reshape(2 * slab_len, 2 * box_edge) / math.sqrt(box_edge)
    forward = np.block([[cos.T, -sin.T], [sin.T, cos.T]]) / math.sqrt(slab_len)
    return jnp.asarray(inverse, BF16), jnp.asarray(forward, BF16)


def dot_nt(left, right):
    return lax.dot_general(left, right, (((1,), (1,)), ((), ())), preferred_element_type=F32)


def dot_tn(left, right):
    return lax.dot_general(left, right, (((0,), (0,)), ((), ())), preferred_element_type=F32)


def dot_nn(left, right):
    return jnp.dot(left, right, preferred_element_type=F32)


def own_sphere(sticks_ref, stick_dev, box_edge):
    middle = box_edge // 2
    start = pl.multiple_of(lax.axis_index("pw") * stick_dev, stick_dev)
    own = sticks_ref[:, pl.ds(start, stick_dev)] - middle
    own = (own * own).astype(F32)
    radial = own[0:1] + own[1:2]
    column = jnp.broadcast_to(radial, (8, stick_dev)).T[:, 0:1]
    level = lax.broadcasted_iota(jnp.int32, (1, box_edge), 1) - middle
    return column + (level * level).astype(F32) < float(middle * middle)


def head_kernel(
    mates,
    coeffs_hbm,
    sticks_hbm,
    table_hbm,
    pot_hbm,
    fwd_hbm,
    tr_hbm,
    out_ref,
    hot_a,
    hot_b,
    pot_ref,
    fwd_ref,
    tr_ref,
    coeffs_ref,
    sticks_ref,
    table_ref,
    sems,
):
    side, n_half = fwd_hbm.shape[1], tr_hbm.shape[1]
    pairs = [
        (sticks_hbm, sticks_ref),
        (coeffs_hbm, coeffs_ref),
        (table_hbm, table_ref),
        (fwd_hbm, fwd_ref.at[:, :side]),
        (tr_hbm, tr_ref.at[:, :n_half]),
        (pot_hbm, pot_ref),
    ]
    copies = [pltpu.make_async_copy(src, dst, sems.at[n]) for n, (src, dst) in enumerate(pairs)]
    for copy in copies:
        copy.start()
    _, stick_dev, box_edge = coeffs_ref.shape
    slab_len = table_ref.shape[0] // 2
    copies[0].wait()
    sphere = own_sphere(sticks_ref, stick_dev, box_edge)
    copies[1].wait()
    copies[2].wait()
    masked = [jnp.where(sphere, coeffs_ref[c].astype(F32), 0.0).astype(BF16) for c in range(2)]
    masked = jnp.concatenate(masked, axis=1)
    rows = dot_nt(table_ref[...], masked).astype(BF16).astype(F32)
    for z in range(slab_len):
        for b in range(mates):
            out_ref[place_of(z, b, slab_len, mates)] = rows[2 * z : 2 * z + 2]

    codes = sticks_ref[...]
    codes = ((codes & 1) * side + (codes >> 1)).astype(F32).astype(BF16)
    rows = lax.broadcasted_iota(jnp.int32, (box_edge, stick_dev), 0).astype(F32).astype(BF16)
    one, none = jnp.ones((), BF16), jnp.zeros((), BF16)
    for at in range(0, codes.shape[1], stick_dev):
        cols = slice(at, at + stick_dev)
        hot_a[:, cols] = jnp.where(rows == codes[0:1, cols], one, none)
        hot_b[:, cols] = jnp.where(rows == codes[1:2, cols], one, none)
    for copy in copies[3:5]:
        copy.wait()
    for p in range(2):
        fwd_ref[p, side:, :n_half] = -fwd_ref[p, :side, n_half:]
        fwd_ref[p, side:, n_half:] = fwd_ref[p, :side, :n_half]
        tr_ref[p, n_half:, :side] = -tr_ref[p, :n_half, side:]
        tr_ref[p, n_half:, side:] = tr_ref[p, :n_half, :side]
    copies[5].wait()


def plane_kernel(
    mates,
    recv_ref,
    hot_a,
    hot_b,
    pot_ref,
    fwd_ref,
    tr_ref,
    out_ref,
    back_ref,
    zeds_ref,
    spread,
    half_ref,
    mid_ref,
    cell_ref,
):
    box_edge, sticks = hot_a.shape
    side = box_edge // 2
    groups = recv_ref.shape[0] // mates
    per = sticks // groups
    grid_len = pot_ref.shape[0]
    n_half = grid_len // 2

    own_mate = lax.rem(lax.axis_index("band"), mates)
    for g in range(groups):
        cols = slice(g * per, (g + 1) * per)
        own = recv_ref[place_of(g, own_mate, groups, mates)].astype(BF16)
        for c in range(2):
            placed = hot_b[:, cols] * own[c : c + 1]
            for p in range(2):
                row = p * box_edge + c * side
                spread[row : row + side, cols] = placed[p * side : (p + 1) * side]

    box = dot_nt(hot_a[...], spread[...]).astype(BF16)
    even = dot_nn(box[:, :box_edge], fwd_ref[0])
    odd = dot_nn(box[:, box_edge:], fwd_ref[1])
    low = (even + odd).astype(BF16)
    high = (even - odd).astype(BF16)
    for p in range(2):
        rows = slice(p * side, (p + 1) * side)
        for c in range(2):
            cols = slice(c * n_half, (c + 1) * n_half)
            half_ref[p, c * side : (c + 1) * side, :n_half] = low[rows, cols]
            half_ref[p, c * side : (c + 1) * side, n_half:] = high[rows, cols]

    step = 256
    for x0 in range(0, n_half, step):
        sums = {}
        for c in range(2):
            rows = slice(c * n_half + x0, c * n_half + x0 + step)
            even = dot_nn(tr_ref[0, rows], half_ref[0])
            odd = dot_nn(tr_ref[1, rows], half_ref[1])
            near = (even + odd) * pot_ref[x0 : x0 + step].astype(F32)
            far = (even - odd) * pot_ref[n_half + x0 : n_half + x0 + step].astype(F32)
            for p, both in ((0, near + far), (1, near - far)):
                sums[p, 0, c] = (both[:, :n_half] + both[:, n_half:]).astype(BF16)
                sums[p, 1, c] = (both[:, :n_half] - both[:, n_half:]).astype(BF16)
        for p in range(2):
            for q in range(2):
                left = jnp.concatenate([sums[p, q, 0], sums[p, q, 1]], axis=1)
                mid = dot_nn(left, tr_ref[q]).astype(BF16)
                for c in range(2):
                    mid_ref[p, c * n_half + x0 : c * n_half + x0 + step, q * side : (q + 1) * side] = mid[
                        :, c * side : (c + 1) * side
                    ]

    for p in range(2):
        cell = dot_nn(fwd_ref[p], mid_ref[p]) * (float(box_edge) / float(grid_len))
        cell_ref[p * box_edge : (p + 1) * box_edge] = cell.astype(BF16)


    wide = 256
    for s0 in range(0, sticks, wide):
        cols = slice(s0, s0 + wide)
        picked = dot_nn(cell_ref[...], hot_b[:, cols])
        parts = []
        for c in range(2):
            value = None
            for p in range(2):
                at = p * box_edge + c * side
                term = picked[at : at + side] * hot_a[p * side : (p + 1) * side, cols].astype(F32)
                value = term if value is None else value + term
            parts.append(jnp.sum(value, axis=0, keepdims=True))
        back = jnp.concatenate(parts, axis=0).astype(BF16).astype(F32)
        back_ref[:, cols] = back
        for g in range(s0 // per, (s0 + wide) // per):
            for b in range(mates):
                out_ref[place_of(g, b, groups, mates), 0:2] = back[:, g * per - s0 : (g + 1) * per - s0]
    gather_rows(mates, recv_ref, zeds_ref)


def gather_rows(mates, recv_ref, rows_ref):
    groups, per = recv_ref.shape[0] // mates, recv_ref.shape[2]
    for g in range(groups):
        for b in range(mates):
            rows_ref[2 * b : 2 * b + 2, g * per : (g + 1) * per] = recv_ref[place_of(g, b, groups, mates)]
    rows_ref[2 * mates :] = jnp.zeros((8 - 2 * mates, rows_ref.shape[1]), F32)


def pair_kernel(mates, count, blocks_ref, back_ref, zeds_ref, *refs):
    others, out_ref, all_zeds = refs[: count - 1], refs[count - 1], refs[count]
    del blocks_ref
    sticks = back_ref.shape[1]
    here = lax.axis_index("band") // mates
    all_zeds[here] = zeds_ref[...]
    for s in range(1, count):
        gather_rows(mates, others[s - 1], all_zeds.at[lax.rem(here - s + count, count)])
    lanes = 8 * count
    total = dot_nt(back_ref[...].astype(BF16), all_zeds[...].reshape(lanes, sticks).astype(BF16))
    for block in range(out_ref.shape[0]):
        out_ref[block, 2:4, :lanes] = total
        out_ref[block, 2:4, lanes:] = jnp.zeros((2, out_ref.shape[2] - lanes), F32)


def tail_kernel(mates, scale, recv_ref, sticks_ref, table_ref, out_hbm, corr_hbm, out_ref, corr_ref, sems):
    blocks, _, stick_dev = recv_ref.shape
    groups = blocks // mates
    own_mate = lax.rem(lax.axis_index("band"), mates)
    box_edge = out_ref.shape[2]
    own = [recv_ref[place_of(g, own_mate, groups, mates)] for g in range(groups)]
    total = own[0][2:4]
    for part in own[1:]:
        total = total + part[2:4]
    total = total * scale
    for q in range(corr_ref.shape[2] // mates):
        for b in range(mates):
            re, im, at = 8 * q + 2 * b, 8 * q + 2 * b + 1, q * mates + b
            corr_ref[0, :, at : at + 1] = total[0:1, re : re + 1] + total[1:2, im : im + 1]
            corr_ref[1, :, at : at + 1] = total[1:2, re : re + 1] - total[0:1, im : im + 1]
    corr_copy = pltpu.make_async_copy(corr_ref, corr_hbm, sems.at[2])
    corr_copy.start()
    sphere = own_sphere(sticks_ref, stick_dev, box_edge)
    back = jnp.concatenate([part[c : c + 1] for c in range(2) for part in own], axis=0).astype(BF16)
    copies = []
    for c in range(2):
        values = dot_tn(back, table_ref[:, c * box_edge : (c + 1) * box_edge])
        out_ref[c] = jnp.where(sphere, values, 0.0).astype(BF16)
        copies.append(pltpu.make_async_copy(out_ref.at[c], out_hbm.at[c], sems.at[c]))
        copies[-1].start()
    for copy in copies:
        copy.wait()
    corr_copy.wait()


def local(band_coeffs, potential, stick_list):
    groups = lax.axis_size("pw")
    bands = lax.axis_size("band")
    _, _, stick_dev, box_edge = band_coeffs.shape
    grid_len = potential.shape[1]
    slab_len = potential.shape[0] * groups
    sticks = stick_list.shape[0]
    columns = stick_list.T
    fwd, transposed = plane_tables(box_edge, grid_len)
    z_inverse, z_forward = z_tables(box_edge, slab_len, grid_len)
    in_hbm = functools.partial(pltpu.with_memory_space_constraint, memory_space=pltpu.HBM)
    hbm, vmem = pl.BlockSpec(memory_space=pltpu.HBM), pl.BlockSpec(memory_space=pltpu.VMEM)
    mates = 2 if bands % 2 == 0 else 1
    count = bands // mates

    send, *operands = pl.pallas_call(
        functools.partial(head_kernel, mates),
        out_shape=[
            jax.ShapeDtypeStruct((mates * groups, 2, stick_dev), F32),
            jax.ShapeDtypeStruct((box_edge, sticks), BF16),
            jax.ShapeDtypeStruct((box_edge, sticks), BF16),
            jax.ShapeDtypeStruct((grid_len, grid_len), BF16),
            jax.ShapeDtypeStruct((2, box_edge, grid_len), BF16),
            jax.ShapeDtypeStruct((2, grid_len, box_edge), BF16),
        ],
        in_specs=[hbm] * 6,
        out_specs=[vmem] * 6,
        scratch_shapes=[
            pltpu.VMEM((2, stick_dev, box_edge), BF16),
            pltpu.VMEM((2, sticks), jnp.int32),
            pltpu.VMEM(z_inverse.shape, BF16),
            pltpu.SemaphoreType.DMA((6,)),
        ],
        compiler_params=pltpu.CompilerParams(vmem_limit_bytes=8 << 20),
        name="head",
    )(
        in_hbm(band_coeffs[0]),
        in_hbm(columns),
        in_hbm(z_inverse),
        in_hbm(potential[0]),
        in_hbm(fwd),
        in_hbm(transposed),
    )
    order = [
        [(q * mates + b) * groups + g for g in reversed(range(groups)) for b in reversed(range(mates))]
        for q in range(count)
    ]
    planes = lax.all_to_all(
        send, ("band", "pw"), split_axis=0, concat_axis=0, tiled=True, axis_index_groups=order
    )
    others = [
        lax.ppermute(planes, "band", [(b, (b + s * mates) % bands) for b in range(bands)]) for s in range(1, count)
    ]
    blocks = jax.ShapeDtypeStruct((mates * groups, 4, stick_dev), F32)
    backs, rows, zeds = pl.pallas_call(
        functools.partial(plane_kernel, mates),
        out_shape=[
            blocks,
            jax.ShapeDtypeStruct((2, sticks), F32),
            jax.ShapeDtypeStruct((8, sticks), F32),
        ],
        in_specs=[vmem] * 6,
        out_specs=[vmem] * 3,
        scratch_shapes=[
            pltpu.VMEM((2 * box_edge, sticks), BF16),
            pltpu.VMEM((2, box_edge, grid_len), BF16),
            pltpu.VMEM((2, grid_len, box_edge), BF16),
            pltpu.VMEM((2 * box_edge, box_edge), BF16),
        ],
        compiler_params=pltpu.CompilerParams(vmem_limit_bytes=16 << 20),
        cost_estimate=pl.CostEstimate(flops=1_400_000_000, bytes_accessed=3 << 20, transcendentals=0),
        name="plane",
    )(planes, *operands)
    backs = pl.pallas_call(
        functools.partial(pair_kernel, mates, count),
        out_shape=blocks,
        in_specs=[vmem] * (2 + count),
        out_specs=vmem,
        scratch_shapes=[pltpu.VMEM((count, 8, sticks), F32)],
        input_output_aliases={0: 0},
        compiler_params=pltpu.CompilerParams(vmem_limit_bytes=4 << 20),
        name="pairs",
    )(backs, rows, zeds, *others)
    back = lax.all_to_all(
        backs,
        ("band", "pw"),
        split_axis=0,
        concat_axis=0,
        tiled=True,
        axis_index_groups=order,
    )
    applied, correlation = pl.pallas_call(
        functools.partial(tail_kernel, mates, 1.0 / math.sqrt(slab_len * sticks)),
        out_shape=[
            jax.ShapeDtypeStruct((2, stick_dev, box_edge), BF16),
            jax.ShapeDtypeStruct((2, 1, bands), F32),
        ],
        in_specs=[vmem] * 3,
        out_specs=[hbm] * 2,
        scratch_shapes=[
            pltpu.VMEM((2, stick_dev, box_edge), BF16),
            pltpu.VMEM((2, 1, bands), F32),
            pltpu.SemaphoreType.DMA((3,)),
        ],
        compiler_params=pltpu.CompilerParams(vmem_limit_bytes=4 << 20),
        name="tail",
    )(back, columns, z_forward)
    return applied[None], correlation.transpose(0, 2, 1)


def solution(mesh):
    return jax.shard_map(
        local,
        mesh=mesh,
        in_specs=(P("band", None, "pw", None), P("pw", None, None), P()),
        out_specs=(P("band", None, "pw", None), P(None, None, "band")),
        check_vma=False,
    )
```

```python
import functools
import math

import jax
import jax.numpy as jnp
import numpy as np
from jax import lax
from jax.experimental import pallas as pl
from jax.experimental.pallas import tpu as pltpu
from jax.sharding import PartitionSpec as P

F32 = jnp.float32
BF16 = jnp.bfloat16


def first_place(group, groups):
    return ((groups - 3) - group) % groups


def place_of(group, mate, groups, mates):
    return (groups - 1 - group) % groups * mates + mates - 1 - mate


def side_of(mates):
    band = lax.axis_index("band")
    return lax.rem(lax.rem(band, mates) + (mates - 1) * (band // mates), mates)


def lead_pair(side, mates):
    return side % mates


def phases(box_index, grid_index, period, factor):
    turns = box_index[:, None] * grid_index[None, :] % period
    angles = turns * (2.0 * math.pi / period)
    return np.cos(angles) * factor, np.sin(angles) * factor


def plane_tables(box_edge, grid_len):
    half = grid_len // 2
    mats = []
    for parity in range(2):
        cos, sin = phases(
            np.arange(parity, box_edge, 2) - box_edge // 2, np.arange(half), grid_len, 1.0 / math.sqrt(box_edge)
        )
        mats.append(np.block([[cos, sin], [-sin, cos]]))
    mats = np.stack(mats)
    return jnp.asarray(mats[:, : box_edge // 2], BF16), jnp.asarray(mats.transpose(0, 2, 1)[:, :half], BF16)


def z_tables(box_edge, slab_len, grid_len):
    cos, sin = phases(np.arange(box_edge) - box_edge // 2, np.arange(slab_len), grid_len, 1.0)
    inverse = np.stack([np.concatenate([cos.T, -sin.T], 1), np.concatenate([sin.T, cos.T], 1)], 1)
    inverse = inverse.reshape(2 * slab_len, 2 * box_edge) / math.sqrt(box_edge)
    forward = np.block([[cos.T, -sin.T], [sin.T, cos.T]]) / math.sqrt(slab_len)
    return jnp.asarray(inverse, BF16), jnp.asarray(forward, BF16)


def dot_nt(left, right):
    return lax.dot_general(left, right, (((1,), (1,)), ((), ())), preferred_element_type=F32)


def dot_tn(left, right):
    return lax.dot_general(left, right, (((0,), (0,)), ((), ())), preferred_element_type=F32)


def dot_nn(left, right):
    return jnp.dot(left, right, preferred_element_type=F32)


def own_sphere(sticks_ref, stick_dev, box_edge):
    middle = box_edge // 2
    start = pl.multiple_of(lax.axis_index("pw") * stick_dev, stick_dev)
    own = sticks_ref[:, pl.ds(start, stick_dev)] - middle
    own = (own * own).astype(F32)
    radial = own[0:1] + own[1:2]
    column = jnp.broadcast_to(radial, (8, stick_dev)).T[:, 0:1]
    level = lax.broadcasted_iota(jnp.int32, (1, box_edge), 1) - middle
    return column + (level * level).astype(F32) < float(middle * middle)


def head_kernel(
    count,
    coeffs_hbm,
    sticks_hbm,
    table_hbm,
    pot_hbm,
    fwd_hbm,
    tr_hbm,
    out_ref,
    hot_a,
    hot_b,
    pot_ref,
    fwd_ref,
    tr_ref,
    coeffs_ref,
    sticks_ref,
    table_ref,
    sems,
):
    side, n_half = fwd_hbm.shape[1], tr_hbm.shape[1]
    pairs = [
        (sticks_hbm, sticks_ref),
        (coeffs_hbm, coeffs_ref),
        (table_hbm, table_ref),
        (fwd_hbm, fwd_ref.at[:, :side]),
        (tr_hbm, tr_ref.at[:, :n_half]),
        (pot_hbm, pot_ref),
    ]
    copies = [pltpu.make_async_copy(src, dst, sems.at[n]) for n, (src, dst) in enumerate(pairs)]
    for copy in copies:
        copy.start()
    _, stick_dev, box_edge = coeffs_ref.shape
    slab_len = table_ref.shape[0] // 2
    copies[0].wait()
    sphere = own_sphere(sticks_ref, stick_dev, box_edge)
    copies[1].wait()
    copies[2].wait()
    masked = [jnp.where(sphere, coeffs_ref[c].astype(F32), 0.0).astype(BF16) for c in range(2)]
    masked = jnp.concatenate(masked, axis=1)
    rows = dot_nt(table_ref[...], masked).astype(BF16).astype(F32)
    for z in range(slab_len):
        for t in range(count):
            out_ref[first_place(z, slab_len) * count + t] = rows[2 * z : 2 * z + 2]

    codes = sticks_ref[...]
    codes = ((codes & 1) * side + (codes >> 1)).astype(F32).astype(BF16)
    rows = lax.broadcasted_iota(jnp.int32, (box_edge, stick_dev), 0).astype(F32).astype(BF16)
    one, none = jnp.ones((), BF16), jnp.zeros((), BF16)
    for at in range(0, codes.shape[1], stick_dev):
        cols = slice(at, at + stick_dev)
        hot_a[:, cols] = jnp.where(rows == codes[0:1, cols], one, none)
        hot_b[:, cols] = jnp.where(rows == codes[1:2, cols], one, none)
    for copy in copies[3:5]:
        copy.wait()
    for p in range(2):
        fwd_ref[p, side:, :n_half] = -fwd_ref[p, :side, n_half:]
        fwd_ref[p, side:, n_half:] = fwd_ref[p, :side, :n_half]
        tr_ref[p, n_half:, :side] = -tr_ref[p, :n_half, side:]
        tr_ref[p, n_half:, side:] = tr_ref[p, :n_half, :side]
    copies[5].wait()


def plane_kernel(
    mates,
    count,
    recv_ref,
    hot_a,
    hot_b,
    pot_ref,
    fwd_ref,
    tr_ref,
    out_ref,
    back_ref,
    zeds_ref,
    spread,
    half_ref,
    mid_ref,
    cell_ref,
):
    box_edge, sticks = hot_a.shape
    side = box_edge // 2
    groups = recv_ref.shape[0] // count
    per = sticks // groups
    grid_len = pot_ref.shape[0]
    n_half = grid_len // 2

    own_place = lax.rem(lax.axis_index("band") // mates - lead_pair(side_of(mates), mates) + count, count)
    for g in range(groups):
        cols = slice(g * per, (g + 1) * per)
        own = recv_ref[first_place(g, groups) * count + own_place].astype(BF16)
        for c in range(2):
            placed = hot_b[:, cols] * own[c : c + 1]
            for p in range(2):
                row = p * box_edge + c * side
                spread[row : row + side, cols] = placed[p * side : (p + 1) * side]

    box = dot_nt(hot_a[...], spread[...]).astype(BF16)
    even = dot_nn(box[:, :box_edge], fwd_ref[0])
    odd = dot_nn(box[:, box_edge:], fwd_ref[1])
    low = (even + odd).astype(BF16)
    high = (even - odd).astype(BF16)
    for p in range(2):
        rows = slice(p * side, (p + 1) * side)
        for c in range(2):
            cols = slice(c * n_half, (c + 1) * n_half)
            half_ref[p, c * side : (c + 1) * side, :n_half] = low[rows, cols]
            half_ref[p, c * side : (c + 1) * side, n_half:] = high[rows, cols]

    step = 256
    for x0 in range(0, n_half, step):
        sums = {}
        for c in range(2):
            rows = slice(c * n_half + x0, c * n_half + x0 + step)
            even = dot_nn(tr_ref[0, rows], half_ref[0])
            odd = dot_nn(tr_ref[1, rows], half_ref[1])
            near = (even + odd) * pot_ref[x0 : x0 + step].astype(F32)
            far = (even - odd) * pot_ref[n_half + x0 : n_half + x0 + step].astype(F32)
            for p, both in ((0, near + far), (1, near - far)):
                sums[p, 0, c] = (both[:, :n_half] + both[:, n_half:]).astype(BF16)
                sums[p, 1, c] = (both[:, :n_half] - both[:, n_half:]).astype(BF16)
        for p in range(2):
            for q in range(2):
                left = jnp.concatenate([sums[p, q, 0], sums[p, q, 1]], axis=1)
                mid = dot_nn(left, tr_ref[q]).astype(BF16)
                for c in range(2):
                    mid_ref[p, c * n_half + x0 : c * n_half + x0 + step, q * side : (q + 1) * side] = mid[
                        :, c * side : (c + 1) * side
                    ]

    for p in range(2):
        cell = dot_nn(fwd_ref[p], mid_ref[p]) * (float(box_edge) / float(grid_len))
        cell_ref[p * box_edge : (p + 1) * box_edge] = cell.astype(BF16)


    wide = 256
    for s0 in range(0, sticks, wide):
        cols = slice(s0, s0 + wide)
        picked = dot_nn(cell_ref[...], hot_b[:, cols])
        parts = []
        for c in range(2):
            value = None
            for p in range(2):
                at = p * box_edge + c * side
                term = picked[at : at + side] * hot_a[p * side : (p + 1) * side, cols].astype(F32)
                value = term if value is None else value + term
            parts.append(jnp.sum(value, axis=0, keepdims=True))
        back = jnp.concatenate(parts, axis=0).astype(BF16).astype(F32)
        back_ref[:, cols] = back
        for g in range(s0 // per, (s0 + wide) // per):
            for b in range(mates):
                out_ref[place_of(g, b, groups, mates), 0:2] = back[:, g * per - s0 : (g + 1) * per - s0]
    zeds_ref[...] = jnp.zeros_like(zeds_ref)
    gather_rows(count, 0, recv_ref, zeds_ref)


def gather_rows(count, shift, recv_ref, rows_ref):
    groups, per = recv_ref.shape[0] // count, recv_ref.shape[2]
    for t in range(count):
        row = shift * count + t
        for g in range(groups):
            block = recv_ref[first_place(g, groups) * count + t]
            for c in range(2):
                at = (c * groups + g) * per
                rows_ref[row : row + 1, at : at + per] = block[c : c + 1]


def pair_kernel(mates, count, blocks_ref, seen_ref, back_ref, *refs):
    others, out_ref, zeds_ref = refs[: mates - 1], refs[mates - 1], refs[mates]
    del blocks_ref, seen_ref
    for s in range(1, mates):
        gather_rows(count, s, others[s - 1], zeds_ref)
    back = back_ref[...].astype(BF16)
    left = jnp.concatenate(
        [jnp.concatenate([back[0:1], back[1:2]], axis=1), jnp.concatenate([back[1:2], -back[0:1]], axis=1)], axis=0
    )
    total = dot_nt(left, zeds_ref[...].astype(BF16))
    bands = mates * count
    for block in range(out_ref.shape[0]):
        out_ref[block, 2:4, :bands] = total[:, :bands]
        out_ref[block, 2:4, bands:] = jnp.zeros((2, out_ref.shape[2] - bands), F32)


def tail_kernel(mates, scale, recv_ref, sticks_ref, table_ref, out_hbm, corr_hbm, out_ref, corr_ref, sems):
    blocks, _, stick_dev = recv_ref.shape
    groups = blocks // mates
    own_mate = lax.rem(lax.axis_index("band"), mates)
    box_edge = out_ref.shape[2]
    own = [recv_ref[place_of(g, own_mate, groups, mates)] for g in range(groups)]
    total = own[0][2:4]
    for part in own[1:]:
        total = total + part[2:4]
    total = total * scale
    side = side_of(mates)
    count = corr_ref.shape[2] // mates
    for q in range(count):
        for b in range(mates):
            group, at = (b - q) % mates, q * mates + b
            column = None
            for k in range(mates):
                row = (k - group) % mates * count + (q - lead_pair(group, mates)) % count
                here = total[:, row : row + 1]
                column = here if column is None else jnp.where(side == k, here, column)
            for c in range(2):
                corr_ref[c, :, at : at + 1] = column[c : c + 1]
    corr_copy = pltpu.make_async_copy(corr_ref, corr_hbm, sems.at[2])
    corr_copy.start()
    sphere = own_sphere(sticks_ref, stick_dev, box_edge)
    back = jnp.concatenate([part[c : c + 1] for c in range(2) for part in own], axis=0).astype(BF16)
    copies = []
    for c in range(2):
        values = dot_tn(back, table_ref[:, c * box_edge : (c + 1) * box_edge])
        out_ref[c] = jnp.where(sphere, values, 0.0).astype(BF16)
        copies.append(pltpu.make_async_copy(out_ref.at[c], out_hbm.at[c], sems.at[c]))
        copies[-1].start()
    for copy in copies:
        copy.wait()
    corr_copy.wait()


def local(band_coeffs, potential, stick_list):
    groups = lax.axis_size("pw")
    bands = lax.axis_size("band")
    _, _, stick_dev, box_edge = band_coeffs.shape
    grid_len = potential.shape[1]
    slab_len = potential.shape[0] * groups
    sticks = stick_list.shape[0]
    columns = stick_list.T
    fwd, transposed = plane_tables(box_edge, grid_len)
    z_inverse, z_forward = z_tables(box_edge, slab_len, grid_len)
    in_hbm = functools.partial(pltpu.with_memory_space_constraint, memory_space=pltpu.HBM)
    hbm, vmem = pl.BlockSpec(memory_space=pltpu.HBM), pl.BlockSpec(memory_space=pltpu.VMEM)
    mates = 2 if bands % 2 == 0 else 1
    count = bands // mates

    send, *operands = pl.pallas_call(
        functools.partial(head_kernel, count),
        out_shape=[
            jax.ShapeDtypeStruct((count * groups, 2, stick_dev), F32),
            jax.ShapeDtypeStruct((box_edge, sticks), BF16),
            jax.ShapeDtypeStruct((box_edge, sticks), BF16),
            jax.ShapeDtypeStruct((grid_len, grid_len), BF16),
            jax.ShapeDtypeStruct((2, box_edge, grid_len), BF16),
            jax.ShapeDtypeStruct((2, grid_len, box_edge), BF16),
        ],
        in_specs=[hbm] * 6,
        out_specs=[vmem] * 6,
        scratch_shapes=[
            pltpu.VMEM((2, stick_dev, box_edge), BF16),
            pltpu.VMEM((2, sticks), jnp.int32),
            pltpu.VMEM(z_inverse.shape, BF16),
            pltpu.SemaphoreType.DMA((6,)),
        ],
        compiler_params=pltpu.CompilerParams(vmem_limit_bytes=8 << 20),
        name="head",
    )(
        in_hbm(band_coeffs[0]),
        in_hbm(columns),
        in_hbm(z_inverse),
        in_hbm(potential[0]),
        in_hbm(fwd),
        in_hbm(transposed),
    )
    first = [
        [
            (q * mates + (side + q) % mates) * groups + g
            for g in sorted(range(groups), key=lambda g: first_place(g, groups))
            for q in [(lead_pair(side, mates) + t) % count for t in range(count)]
        ]
        for side in range(mates)
    ]
    second = sorted(
        ((g, b) for g in range(groups) for b in range(mates)), key=lambda member: place_of(*member, groups, mates)
    )
    second = [[(q * mates + b) * groups + g for g, b in second] for q in range(count)]
    planes = lax.all_to_all(
        send, ("band", "pw"), split_axis=0, concat_axis=0, tiled=True, axis_index_groups=first
    )
    others = [
        lax.ppermute(planes, "band", [(b, b - b % mates + (b + s) % mates) for b in range(bands)])
        for s in range(1, mates)
    ]
    span = -(-bands // 8) * 8
    blocks = jax.ShapeDtypeStruct((mates * groups, 4, stick_dev), F32)
    backs, rows, zeds = pl.pallas_call(
        functools.partial(plane_kernel, mates, count),
        out_shape=[
            blocks,
            jax.ShapeDtypeStruct((2, sticks), F32),
            jax.ShapeDtypeStruct((span, 2 * sticks), F32),
        ],
        in_specs=[vmem] * 6,
        out_specs=[vmem] * 3,
        scratch_shapes=[
            pltpu.VMEM((2 * box_edge, sticks), BF16),
            pltpu.VMEM((2, box_edge, grid_len), BF16),
            pltpu.VMEM((2, grid_len, box_edge), BF16),
            pltpu.VMEM((2 * box_edge, box_edge), BF16),
        ],
        compiler_params=pltpu.CompilerParams(vmem_limit_bytes=16 << 20),
        cost_estimate=pl.CostEstimate(flops=1_400_000_000, bytes_accessed=3 << 20, transcendentals=0),
        name="plane",
    )(planes, *operands)
    backs, _ = pl.pallas_call(
        functools.partial(pair_kernel, mates, count),
        out_shape=[blocks, jax.ShapeDtypeStruct((span, 2 * sticks), F32)],
        in_specs=[vmem] * (2 + mates),
        out_specs=[vmem] * 2,
        input_output_aliases={0: 0, 1: 1},
        compiler_params=pltpu.CompilerParams(vmem_limit_bytes=4 << 20),
        name="pairs",
    )(backs, zeds, rows, *others)
    back = lax.all_to_all(
        backs,
        ("band", "pw"),
        split_axis=0,
        concat_axis=0,
        tiled=True,
        axis_index_groups=second,
    )
    applied, correlation = pl.pallas_call(
        functools.partial(tail_kernel, mates, 1.0 / math.sqrt(slab_len * sticks)),
        out_shape=[
            jax.ShapeDtypeStruct((2, stick_dev, box_edge), BF16),
            jax.ShapeDtypeStruct((2, 1, bands), F32),
        ],
        in_specs=[vmem] * 3,
        out_specs=[hbm] * 2,
        scratch_shapes=[
            pltpu.VMEM((2, stick_dev, box_edge), BF16),
            pltpu.VMEM((2, 1, bands), F32),
            pltpu.SemaphoreType.DMA((3,)),
        ],
        compiler_params=pltpu.CompilerParams(vmem_limit_bytes=4 << 20),
        name="tail",
    )(back, columns, z_forward)
    return applied[None], correlation.transpose(0, 2, 1)


def solution(mesh):
    return jax.shard_map(
        local,
        mesh=mesh,
        in_specs=(P("band", None, "pw", None), P("pw", None, None), P()),
        out_specs=(P("band", None, "pw", None), P(None, None, "band")),
        check_vma=False,
    )
```

```python
import functools
import math

import jax
import jax.numpy as jnp
import numpy as np
from jax import lax
from jax.experimental import pallas as pl
from jax.experimental.pallas import tpu as pltpu
from jax.sharding import PartitionSpec as P

F32 = jnp.float32
BF16 = jnp.bfloat16


def first_place(group, groups):
    return ((groups - 3) - group) % groups


def place_of(group, mate, groups, mates):
    return (groups - 1 - group) % groups * mates + mates - 1 - mate


def side_of(mates):
    band = lax.axis_index("band")
    return lax.rem(lax.rem(band, mates) + (mates - 1) * (band // mates), mates)


def lead_pair(side, mates):
    return side % mates


def phases(box_index, grid_index, period, factor):
    turns = box_index[:, None] * grid_index[None, :] % period
    angles = turns * (2.0 * math.pi / period)
    return np.cos(angles) * factor, np.sin(angles) * factor


def plane_tables(box_edge, grid_len):
    half = grid_len // 2
    mats = []
    for parity in range(2):
        cos, sin = phases(
            np.arange(parity, box_edge, 2) - box_edge // 2, np.arange(half), grid_len, 1.0 / math.sqrt(box_edge)
        )
        mats.append(np.block([[cos, sin], [-sin, cos]]))
    mats = np.stack(mats)
    return jnp.asarray(mats[:, : box_edge // 2], BF16), jnp.asarray(mats.transpose(0, 2, 1)[:, :half], BF16)


def z_tables(box_edge, slab_len, grid_len):
    cos, sin = phases(np.arange(box_edge) - box_edge // 2, np.arange(slab_len), grid_len, 1.0)
    inverse = np.stack([np.concatenate([cos.T, -sin.T], 1), np.concatenate([sin.T, cos.T], 1)], 1)
    inverse = inverse.reshape(2 * slab_len, 2 * box_edge) / math.sqrt(box_edge)
    forward = np.block([[cos.T, -sin.T], [sin.T, cos.T]]) / math.sqrt(slab_len)
    return jnp.asarray(inverse, BF16), jnp.asarray(forward, BF16)


def dot_nt(left, right):
    return lax.dot_general(left, right, (((1,), (1,)), ((), ())), preferred_element_type=F32)


def dot_tn(left, right):
    return lax.dot_general(left, right, (((0,), (0,)), ((), ())), preferred_element_type=F32)


def dot_nn(left, right):
    return jnp.dot(left, right, preferred_element_type=F32)


def own_sphere(sticks_ref, stick_dev, box_edge):
    middle = box_edge // 2
    start = pl.multiple_of(lax.axis_index("pw") * stick_dev, stick_dev)
    own = sticks_ref[:, pl.ds(start, stick_dev)] - middle
    own = (own * own).astype(F32)
    radial = own[0:1] + own[1:2]
    column = jnp.broadcast_to(radial, (8, stick_dev)).T[:, 0:1]
    level = lax.broadcasted_iota(jnp.int32, (1, box_edge), 1) - middle
    return column + (level * level).astype(F32) < float(middle * middle)


def head_kernel(
    count,
    coeffs_hbm,
    sticks_hbm,
    table_hbm,
    pot_hbm,
    fwd_hbm,
    tr_hbm,
    out_ref,
    hot_a,
    hot_b,
    pot_ref,
    fwd_ref,
    tr_ref,
    coeffs_ref,
    sticks_ref,
    table_ref,
    sems,
):
    side, n_half = fwd_hbm.shape[1], tr_hbm.shape[1]
    pairs = [
        (sticks_hbm, sticks_ref),
        (coeffs_hbm, coeffs_ref),
        (table_hbm, table_ref),
        (fwd_hbm, fwd_ref.at[:, :side]),
        (tr_hbm, tr_ref.at[:, :n_half]),
        (pot_hbm, pot_ref),
    ]
    copies = [pltpu.make_async_copy(src, dst, sems.at[n]) for n, (src, dst) in enumerate(pairs)]
    for copy in copies:
        copy.start()
    _, stick_dev, box_edge = coeffs_ref.shape
    slab_len = table_ref.shape[0] // 2
    copies[0].wait()
    sphere = own_sphere(sticks_ref, stick_dev, box_edge)
    copies[1].wait()
    copies[2].wait()
    masked = [jnp.where(sphere, coeffs_ref[c].astype(F32), 0.0).astype(BF16) for c in range(2)]
    masked = jnp.concatenate(masked, axis=1)
    rows = dot_nt(table_ref[...], masked).astype(BF16).astype(F32)
    for z in range(slab_len):
        for t in range(count):
            out_ref[first_place(z, slab_len) * count + t] = rows[2 * z : 2 * z + 2]

    codes = sticks_ref[...]
    codes = ((codes & 1) * side + (codes >> 1)).astype(F32).astype(BF16)
    rows = lax.broadcasted_iota(jnp.int32, (box_edge, stick_dev), 0).astype(F32).astype(BF16)
    one, none = jnp.ones((), BF16), jnp.zeros((), BF16)
    for at in range(0, codes.shape[1], stick_dev):
        cols = slice(at, at + stick_dev)
        hot_a[:, cols] = jnp.where(rows == codes[0:1, cols], one, none)
        hot_b[:, cols] = jnp.where(rows == codes[1:2, cols], one, none)
    for copy in copies[3:5]:
        copy.wait()
    for p in range(2):
        fwd_ref[p, side:, :n_half] = -fwd_ref[p, :side, n_half:]
        fwd_ref[p, side:, n_half:] = fwd_ref[p, :side, :n_half]
        tr_ref[p, n_half:, :side] = -tr_ref[p, :n_half, side:]
        tr_ref[p, n_half:, side:] = tr_ref[p, :n_half, :side]
    copies[5].wait()


def plane_kernel(
    mates,
    count,
    recv_ref,
    hot_a,
    hot_b,
    pot_ref,
    fwd_ref,
    tr_ref,
    back_ref,
    zeds_ref,
    spread,
    half_ref,
    wide_ref,
    left_ref,
    mid_ref,
    cell_ref,
):
    box_edge, sticks = hot_a.shape
    side = box_edge // 2
    groups = recv_ref.shape[0] // count
    per = sticks // groups
    grid_len = pot_ref.shape[0]
    n_half = grid_len // 2

    own_place = lax.rem(lax.axis_index("band") // mates - lead_pair(side_of(mates), mates) + count, count)
    for g in range(groups):
        cols = slice(g * per, (g + 1) * per)
        own = recv_ref[first_place(g, groups) * count + own_place].astype(BF16)
        for c in range(2):
            placed = hot_b[:, cols] * own[c : c + 1]
            for p in range(2):
                row = p * box_edge + c * side
                spread[row : row + side, cols] = placed[p * side : (p + 1) * side]

    box = dot_nt(hot_a[...], spread[...]).astype(BF16)
    for p in range(2):
        wide_ref[p] = dot_nn(box[:, p * box_edge : (p + 1) * box_edge], fwd_ref[p])
    for r in range(0, box_edge, 16):
        even, odd = wide_ref[0, r : r + 16], wide_ref[1, r : r + 16]
        p, at = r // side, r % side
        for n, both in enumerate((even + odd, even - odd)):
            both = both.astype(BF16)
            for c in range(2):
                half_ref[p, c * side + at : c * side + at + 16, n * n_half : (n + 1) * n_half] = both[
                    :, c * n_half : (c + 1) * n_half
                ]

    for c in range(2):
        for p in range(2):
            wide_ref[2 * c + p] = dot_nn(tr_ref[p, c * n_half : (c + 1) * n_half], half_ref[p])
    for c in range(2):
        cols = slice(c * n_half, (c + 1) * n_half)
        for r in range(0, n_half, 16):
            rows = slice(r, r + 16)
            even, odd = wide_ref[2 * c, rows], wide_ref[2 * c + 1, rows]
            near = (even + odd) * pot_ref[rows].astype(F32)
            far = (even - odd) * pot_ref[n_half + r : n_half + r + 16].astype(F32)
            for p, both in ((0, near + far), (1, near - far)):
                left_ref[p, 0, rows, cols] = (both[:, :n_half] + both[:, n_half:]).astype(BF16)
                left_ref[p, 1, rows, cols] = (both[:, :n_half] - both[:, n_half:]).astype(BF16)
    for p in range(2):
        for q in range(2):
            mid = dot_nn(left_ref[p, q], tr_ref[q]).astype(BF16)
            for c in range(2):
                mid_ref[p, c * n_half : (c + 1) * n_half, q * side : (q + 1) * side] = mid[
                    :, c * side : (c + 1) * side
                ]

    for p in range(2):
        cell = dot_nn(fwd_ref[p], mid_ref[p]) * (float(box_edge) / float(grid_len))
        cell_ref[p * box_edge : (p + 1) * box_edge] = cell.astype(BF16)

    wide = 256
    for s0 in range(0, sticks, wide):
        cols = slice(s0, s0 + wide)
        picked = dot_nn(cell_ref[...], hot_b[:, cols])
        parts = [None, None]
        for p in range(2):
            for r in range(0, side, 16):
                hot = hot_a[p * side + r : p * side + r + 16, cols].astype(F32)
                for c in range(2):
                    at = p * box_edge + c * side + r
                    term = picked[at : at + 16] * hot
                    term = term[:8] + term[8:]
                    parts[c] = term if parts[c] is None else parts[c] + term
        parts = [jnp.sum(part, axis=0, keepdims=True) for part in parts]
        back = jnp.concatenate(parts, axis=0).astype(BF16).astype(F32)
        back_ref[:, cols] = back
    zeds_ref[...] = jnp.zeros_like(zeds_ref)
    gather_rows(count, 0, recv_ref, zeds_ref)


def gather_rows(count, shift, recv_ref, rows_ref):
    groups, per = recv_ref.shape[0] // count, recv_ref.shape[2]
    for t in range(count):
        row = shift * count + t
        for g in range(groups):
            block = recv_ref[first_place(g, groups) * count + t]
            for c in range(2):
                at = (c * groups + g) * per
                rows_ref[row : row + 1, at : at + per] = block[c : c + 1]


def pair_kernel(mates, count, seen_ref, back_ref, *refs):
    others, out_ref, zeds_ref = refs[: mates - 1], refs[mates - 1], refs[mates]
    zeds_ref[...] = seen_ref[...]
    for s in range(1, mates):
        gather_rows(count, s, others[s - 1], zeds_ref)
    back = back_ref[...].astype(BF16)
    left = jnp.concatenate(
        [jnp.concatenate([back[0:1], back[1:2]], axis=1), jnp.concatenate([back[1:2], -back[0:1]], axis=1)], axis=0
    )
    total = dot_nt(left, zeds_ref[...].astype(BF16))
    bands = mates * count
    blocks, _, per = out_ref.shape
    groups = blocks // mates
    for g in range(groups):
        for b in range(mates):
            at = place_of(g, b, groups, mates)
            out_ref[at, 0:2] = back_ref[:, g * per : (g + 1) * per]
            out_ref[at, 2:4, :bands] = total[:, :bands]
            out_ref[at, 2:4, bands:] = jnp.zeros((2, per - bands), F32)


def tail_kernel(mates, scale, recv_ref, sticks_ref, table_ref, out_hbm, corr_hbm, out_ref, corr_ref, sems):
    blocks, _, stick_dev = recv_ref.shape
    groups = blocks // mates
    own_mate = lax.rem(lax.axis_index("band"), mates)
    box_edge = out_ref.shape[2]
    own = [recv_ref[place_of(g, own_mate, groups, mates)] for g in range(groups)]
    total = own[0][2:4]
    for part in own[1:]:
        total = total + part[2:4]
    total = total * scale
    side = side_of(mates)
    count = corr_ref.shape[2] // mates
    for q in range(count):
        for b in range(mates):
            group, at = (b - q) % mates, q * mates + b
            column = None
            for k in range(mates):
                row = (k - group) % mates * count + (q - lead_pair(group, mates)) % count
                here = total[:, row : row + 1]
                column = here if column is None else jnp.where(side == k, here, column)
            for c in range(2):
                corr_ref[c, :, at : at + 1] = column[c : c + 1]
    corr_copy = pltpu.make_async_copy(corr_ref, corr_hbm, sems.at[2])
    corr_copy.start()
    sphere = own_sphere(sticks_ref, stick_dev, box_edge)
    back = jnp.concatenate([part[c : c + 1] for c in range(2) for part in own], axis=0).astype(BF16)
    copies = []
    for c in range(2):
        values = dot_tn(back, table_ref[:, c * box_edge : (c + 1) * box_edge])
        out_ref[c] = jnp.where(sphere, values, 0.0).astype(BF16)
        copies.append(pltpu.make_async_copy(out_ref.at[c], out_hbm.at[c], sems.at[c]))
        copies[-1].start()
    for copy in copies:
        copy.wait()
    corr_copy.wait()


def local(band_coeffs, potential, stick_list):
    groups = lax.axis_size("pw")
    bands = lax.axis_size("band")
    _, _, stick_dev, box_edge = band_coeffs.shape
    grid_len = potential.shape[1]
    slab_len = potential.shape[0] * groups
    sticks = stick_list.shape[0]
    columns = stick_list.T
    fwd, transposed = plane_tables(box_edge, grid_len)
    z_inverse, z_forward = z_tables(box_edge, slab_len, grid_len)
    in_hbm = functools.partial(pltpu.with_memory_space_constraint, memory_space=pltpu.HBM)
    hbm, vmem = pl.BlockSpec(memory_space=pltpu.HBM), pl.BlockSpec(memory_space=pltpu.VMEM)
    mates = 2 if bands % 2 == 0 else 1
    count = bands // mates

    send, *operands = pl.pallas_call(
        functools.partial(head_kernel, count),
        out_shape=[
            jax.ShapeDtypeStruct((count * groups, 2, stick_dev), F32),
            jax.ShapeDtypeStruct((box_edge, sticks), BF16),
            jax.ShapeDtypeStruct((box_edge, sticks), BF16),
            jax.ShapeDtypeStruct((grid_len, grid_len), BF16),
            jax.ShapeDtypeStruct((2, box_edge, grid_len), BF16),
            jax.ShapeDtypeStruct((2, grid_len, box_edge), BF16),
        ],
        in_specs=[hbm] * 6,
        out_specs=[vmem] * 6,
        scratch_shapes=[
            pltpu.VMEM((2, stick_dev, box_edge), BF16),
            pltpu.VMEM((2, sticks), jnp.int32),
            pltpu.VMEM(z_inverse.shape, BF16),
            pltpu.SemaphoreType.DMA((6,)),
        ],
        compiler_params=pltpu.CompilerParams(vmem_limit_bytes=8 << 20),
        name="head",
    )(
        in_hbm(band_coeffs[0]),
        in_hbm(columns),
        in_hbm(z_inverse),
        in_hbm(potential[0]),
        in_hbm(fwd),
        in_hbm(transposed),
    )
    first = [
        [
            (q * mates + (side + q) % mates) * groups + g
            for g in sorted(range(groups), key=lambda g: first_place(g, groups))
            for q in [(lead_pair(side, mates) + t) % count for t in range(count)]
        ]
        for side in range(mates)
    ]
    second = sorted(
        ((g, b) for g in range(groups) for b in range(mates)), key=lambda member: place_of(*member, groups, mates)
    )
    second = [[(q * mates + b) * groups + g for g, b in second] for q in range(count)]
    planes = lax.all_to_all(
        send, ("band", "pw"), split_axis=0, concat_axis=0, tiled=True, axis_index_groups=first
    )
    others = [
        lax.ppermute(planes, "band", [(b, b - b % mates + (b + s) % mates) for b in range(bands)])
        for s in range(1, mates)
    ]
    span = -(-bands // 8) * 8
    rows, zeds = pl.pallas_call(
        functools.partial(plane_kernel, mates, count),
        out_shape=[
            jax.ShapeDtypeStruct((2, sticks), F32),
            jax.ShapeDtypeStruct((span, 2 * sticks), F32),
        ],
        in_specs=[vmem] * 6,
        out_specs=[vmem] * 2,
        scratch_shapes=[
            pltpu.VMEM((2 * box_edge, sticks), BF16),
            pltpu.VMEM((2, box_edge, grid_len), BF16),
            pltpu.VMEM((4, grid_len // 2, grid_len), F32),
            pltpu.VMEM((2, 2, grid_len // 2, grid_len), BF16),
            pltpu.VMEM((2, grid_len, box_edge), BF16),
            pltpu.VMEM((2 * box_edge, box_edge), BF16),
        ],
        compiler_params=pltpu.CompilerParams(vmem_limit_bytes=16 << 20),
        cost_estimate=pl.CostEstimate(flops=1_400_000_000, bytes_accessed=3 << 20, transcendentals=0),
        name="plane",
    )(planes, *operands)
    backs = pl.pallas_call(
        functools.partial(pair_kernel, mates, count),
        out_shape=jax.ShapeDtypeStruct((mates * groups, 4, stick_dev), F32),
        in_specs=[vmem] * (1 + mates),
        out_specs=vmem,
        scratch_shapes=[pltpu.VMEM((span, 2 * sticks), F32)],
        compiler_params=pltpu.CompilerParams(vmem_limit_bytes=4 << 20),
        name="pairs",
    )(zeds, rows, *others)
    back = lax.all_to_all(
        backs,
        ("band", "pw"),
        split_axis=0,
        concat_axis=0,
        tiled=True,
        axis_index_groups=second,
    )
    applied, correlation = pl.pallas_call(
        functools.partial(tail_kernel, mates, 1.0 / math.sqrt(slab_len * sticks)),
        out_shape=[
            jax.ShapeDtypeStruct((2, stick_dev, box_edge), BF16),
            jax.ShapeDtypeStruct((2, 1, bands), F32),
        ],
        in_specs=[vmem] * 3,
        out_specs=[hbm] * 2,
        scratch_shapes=[
            pltpu.VMEM((2, stick_dev, box_edge), BF16),
            pltpu.VMEM((2, 1, bands), F32),
            pltpu.SemaphoreType.DMA((3,)),
        ],
        compiler_params=pltpu.CompilerParams(vmem_limit_bytes=4 << 20),
        name="tail",
    )(back, columns, z_forward)
    return applied[None], correlation.transpose(0, 2, 1)


def solution(mesh):
    return jax.shard_map(
        local,
        mesh=mesh,
        in_specs=(P("band", None, "pw", None), P("pw", None, None), P()),
        out_specs=(P("band", None, "pw", None), P(None, None, "band")),
        check_vma=False,
    )
```

```python
import functools
import math

import jax
import jax.numpy as jnp
import numpy as np
from jax import lax
from jax.experimental import pallas as pl
from jax.experimental.pallas import tpu as pltpu
from jax.sharding import PartitionSpec as P

F32 = jnp.float32
BF16 = jnp.bfloat16


def first_place(group, groups):
    return ((groups - 3) - group) % groups


def place_of(group, mate, groups, mates):
    return (groups - 1 - group) % groups * mates + mates - 1 - mate


def side_of(mates):
    band = lax.axis_index("band")
    return lax.rem(lax.rem(band, mates) + (mates - 1) * (band // mates), mates)


def lead_pair(side, mates):
    return side % mates


def phases(box_index, grid_index, period, factor):
    turns = box_index[:, None] * grid_index[None, :] % period
    angles = turns * (2.0 * math.pi / period)
    return np.cos(angles) * factor, np.sin(angles) * factor


def plane_tables(box_edge, grid_len):
    half = grid_len // 2
    mats = []
    for parity in range(2):
        cos, sin = phases(
            np.arange(parity, box_edge, 2) - box_edge // 2, np.arange(half), grid_len, 1.0 / math.sqrt(box_edge)
        )
        mats.append(np.block([[cos, sin], [-sin, cos]]))
    mats = np.stack(mats)
    return jnp.asarray(mats[:, : box_edge // 2], BF16), jnp.asarray(mats.transpose(0, 2, 1)[:, :half], BF16)


def z_tables(box_edge, slab_len, grid_len):
    cos, sin = phases(np.arange(box_edge) - box_edge // 2, np.arange(slab_len), grid_len, 1.0)
    inverse = np.stack([np.concatenate([cos.T, -sin.T], 1), np.concatenate([sin.T, cos.T], 1)], 1)
    inverse = inverse.reshape(2 * slab_len, 2 * box_edge) / math.sqrt(box_edge)
    forward = np.block([[cos.T, -sin.T], [sin.T, cos.T]]) / math.sqrt(slab_len)
    return jnp.asarray(inverse, BF16), jnp.asarray(forward, BF16)


def dot_nt(left, right):
    return lax.dot_general(left, right, (((1,), (1,)), ((), ())), preferred_element_type=F32)


def dot_tn(left, right):
    return lax.dot_general(left, right, (((0,), (0,)), ((), ())), preferred_element_type=F32)


def dot_nn(left, right):
    return jnp.dot(left, right, preferred_element_type=F32)


def own_sphere(sticks_ref, stick_dev, box_edge):
    middle = box_edge // 2
    start = pl.multiple_of(lax.axis_index("pw") * stick_dev, stick_dev)
    own = sticks_ref[:, pl.ds(start, stick_dev)] - middle
    own = (own * own).astype(F32)
    radial = own[0:1] + own[1:2]
    column = jnp.broadcast_to(radial, (8, stick_dev)).T[:, 0:1]
    level = lax.broadcasted_iota(jnp.int32, (1, box_edge), 1) - middle
    return column + (level * level).astype(F32) < float(middle * middle)


def head_kernel(
    count,
    coeffs_hbm,
    sticks_hbm,
    table_hbm,
    pot_hbm,
    fwd_hbm,
    tr_hbm,
    out_ref,
    hot_a,
    hot_b,
    pot_ref,
    fwd_ref,
    tr_ref,
    coeffs_ref,
    sticks_ref,
    table_ref,
    sems,
):
    side, n_half = fwd_hbm.shape[1], tr_hbm.shape[1]
    pairs = [
        (sticks_hbm, sticks_ref),
        (coeffs_hbm, coeffs_ref),
        (table_hbm, table_ref),
        (fwd_hbm, fwd_ref.at[:, :side]),
        (tr_hbm, tr_ref.at[:, :n_half]),
        (pot_hbm, pot_ref),
    ]
    copies = [pltpu.make_async_copy(src, dst, sems.at[n]) for n, (src, dst) in enumerate(pairs)]
    for n, copy in enumerate(copies):
        copy.start(priority=n // 3)
    _, stick_dev, box_edge = coeffs_ref.shape
    slab_len = table_ref.shape[0] // 2
    copies[0].wait()
    sphere = own_sphere(sticks_ref, stick_dev, box_edge)
    copies[1].wait()
    copies[2].wait()
    masked = [jnp.where(sphere, coeffs_ref[c].astype(F32), 0.0).astype(BF16) for c in range(2)]
    masked = jnp.concatenate(masked, axis=1)
    rows = dot_nt(table_ref[...], masked).astype(BF16).astype(F32)
    for z in range(slab_len):
        for t in range(count):
            out_ref[first_place(z, slab_len) * count + t] = rows[2 * z : 2 * z + 2]

    codes = sticks_ref[...]
    codes = ((codes & 1) * side + (codes >> 1)).astype(F32).astype(BF16)
    rows = lax.broadcasted_iota(jnp.int32, (box_edge, stick_dev), 0).astype(F32).astype(BF16)
    one, none = jnp.ones((), BF16), jnp.zeros((), BF16)
    for at in range(0, codes.shape[1], stick_dev):
        cols = slice(at, at + stick_dev)
        hot_a[:, cols] = jnp.where(rows == codes[0:1, cols], one, none)
        hot_b[:, cols] = jnp.where(rows == codes[1:2, cols], one, none)
    for copy in copies[3:5]:
        copy.wait()
    for p in range(2):
        fwd_ref[p, side:, :n_half] = -fwd_ref[p, :side, n_half:]
        fwd_ref[p, side:, n_half:] = fwd_ref[p, :side, :n_half]
        tr_ref[p, n_half:, :side] = -tr_ref[p, :n_half, side:]
        tr_ref[p, n_half:, side:] = tr_ref[p, :n_half, :side]
    copies[5].wait()


def plane_kernel(
    mates,
    count,
    recv_ref,
    hot_a,
    hot_b,
    pot_ref,
    fwd_ref,
    tr_ref,
    back_ref,
    zeds_ref,
    spread,
    half_ref,
    wide_ref,
    left_ref,
    mid_ref,
    cell_ref,
):
    box_edge, sticks = hot_a.shape
    side = box_edge // 2
    groups = recv_ref.shape[0] // count
    per = sticks // groups
    grid_len = pot_ref.shape[0]
    n_half = grid_len // 2

    own_place = lax.rem(lax.axis_index("band") // mates - lead_pair(side_of(mates), mates) + count, count)
    for g in range(groups):
        cols = slice(g * per, (g + 1) * per)
        own = recv_ref[first_place(g, groups) * count + own_place].astype(BF16)
        for c in range(2):
            placed = hot_b[:, cols] * own[c : c + 1]
            for p in range(2):
                row = p * box_edge + c * side
                spread[row : row + side, cols] = placed[p * side : (p + 1) * side]

    box = dot_nt(hot_a[...], spread[...]).astype(BF16)
    for p in range(2):
        wide_ref[p] = dot_nn(box[:, p * box_edge : (p + 1) * box_edge], fwd_ref[p])
    for r in range(0, box_edge, 16):
        even, odd = wide_ref[0, r : r + 16], wide_ref[1, r : r + 16]
        p, at = r // side, r % side
        for n, both in enumerate((even + odd, even - odd)):
            both = both.astype(BF16)
            for c in range(2):
                half_ref[p, c * side + at : c * side + at + 16, n * n_half : (n + 1) * n_half] = both[
                    :, c * n_half : (c + 1) * n_half
                ]

    for c in range(2):
        for p in range(2):
            wide_ref[2 * c + p] = dot_nn(tr_ref[p, c * n_half : (c + 1) * n_half], half_ref[p])
    for c in range(2):
        cols = slice(c * n_half, (c + 1) * n_half)
        for r in range(0, n_half, 16):
            rows = slice(r, r + 16)
            even, odd = wide_ref[2 * c, rows], wide_ref[2 * c + 1, rows]
            near = (even + odd) * pot_ref[rows].astype(F32)
            far = (even - odd) * pot_ref[n_half + r : n_half + r + 16].astype(F32)
            for p, both in ((0, near + far), (1, near - far)):
                left_ref[p, 0, rows, cols] = (both[:, :n_half] + both[:, n_half:]).astype(BF16)
                left_ref[p, 1, rows, cols] = (both[:, :n_half] - both[:, n_half:]).astype(BF16)
    for p in range(2):
        for q in range(2):
            mid = dot_nn(left_ref[p, q], tr_ref[q]).astype(BF16)
            for c in range(2):
                mid_ref[p, c * n_half : (c + 1) * n_half, q * side : (q + 1) * side] = mid[
                    :, c * side : (c + 1) * side
                ]

    for p in range(2):
        cell = dot_nn(fwd_ref[p], mid_ref[p]) * (float(box_edge) / float(grid_len))
        cell_ref[p * box_edge : (p + 1) * box_edge] = cell.astype(BF16)

    wide = 256
    for s0 in range(0, sticks, wide):
        cols = slice(s0, s0 + wide)
        picked = dot_nn(cell_ref[...], hot_b[:, cols])
        parts = [None, None]
        for p in range(2):
            for r in range(0, side, 16):
                hot = hot_a[p * side + r : p * side + r + 16, cols].astype(F32)
                for c in range(2):
                    at = p * box_edge + c * side + r
                    term = picked[at : at + 16] * hot
                    term = term[:8] + term[8:]
                    parts[c] = term if parts[c] is None else parts[c] + term
        parts = [jnp.sum(part, axis=0, keepdims=True) for part in parts]
        back = jnp.concatenate(parts, axis=0).astype(BF16).astype(F32)
        back_ref[:, cols] = back
    zeds_ref[...] = jnp.zeros_like(zeds_ref)
    gather_rows(count, 0, recv_ref, zeds_ref)


def gather_rows(count, shift, recv_ref, rows_ref):
    groups, per = recv_ref.shape[0] // count, recv_ref.shape[2]
    for t in range(count):
        row = shift * count + t
        for g in range(groups):
            block = recv_ref[first_place(g, groups) * count + t]
            for c in range(2):
                at = (c * groups + g) * per
                rows_ref[row : row + 1, at : at + per] = block[c : c + 1]


def pair_kernel(mates, count, seen_ref, back_ref, *refs):
    others, out_ref, zeds_ref = refs[: mates - 1], refs[mates - 1], refs[mates]
    zeds_ref[...] = seen_ref[...]
    for s in range(1, mates):
        gather_rows(count, s, others[s - 1], zeds_ref)
    back = back_ref[...].astype(BF16)
    left = jnp.concatenate(
        [jnp.concatenate([back[0:1], back[1:2]], axis=1), jnp.concatenate([back[1:2], -back[0:1]], axis=1)], axis=0
    )
    total = dot_nt(left, zeds_ref[...].astype(BF16))
    bands = mates * count
    blocks, _, per = out_ref.shape
    groups = blocks // mates
    for g in range(groups):
        for b in range(mates):
            at = place_of(g, b, groups, mates)
            out_ref[at, 0:2] = back_ref[:, g * per : (g + 1) * per]
            out_ref[at, 2:4, :bands] = total[:, :bands]
            out_ref[at, 2:4, bands:] = jnp.zeros((2, per - bands), F32)


def tail_kernel(mates, scale, recv_ref, sticks_ref, table_ref, out_hbm, corr_hbm, out_ref, corr_ref, sems):
    blocks, _, stick_dev = recv_ref.shape
    groups = blocks // mates
    own_mate = lax.rem(lax.axis_index("band"), mates)
    box_edge = out_ref.shape[2]
    own = [recv_ref[place_of(g, own_mate, groups, mates)] for g in range(groups)]
    total = own[0][2:4]
    for part in own[1:]:
        total = total + part[2:4]
    total = total * scale
    side = side_of(mates)
    count = corr_ref.shape[2] // mates
    for q in range(count):
        for b in range(mates):
            group, at = (b - q) % mates, q * mates + b
            column = None
            for k in range(mates):
                row = (k - group) % mates * count + (q - lead_pair(group, mates)) % count
                here = total[:, row : row + 1]
                column = here if column is None else jnp.where(side == k, here, column)
            for c in range(2):
                corr_ref[c, :, at : at + 1] = column[c : c + 1]
    corr_copy = pltpu.make_async_copy(corr_ref, corr_hbm, sems.at[2])
    corr_copy.start()
    sphere = own_sphere(sticks_ref, stick_dev, box_edge)
    back = jnp.concatenate([part[c : c + 1] for c in range(2) for part in own], axis=0).astype(BF16)
    copies = []
    for c in range(2):
        values = dot_tn(back, table_ref[:, c * box_edge : (c + 1) * box_edge])
        out_ref[c] = jnp.where(sphere, values, 0.0).astype(BF16)
        copies.append(pltpu.make_async_copy(out_ref.at[c], out_hbm.at[c], sems.at[c]))
        copies[-1].start()
    for copy in copies:
        copy.wait()
    corr_copy.wait()


def local(band_coeffs, potential, stick_list):
    groups = lax.axis_size("pw")
    bands = lax.axis_size("band")
    _, _, stick_dev, box_edge = band_coeffs.shape
    grid_len = potential.shape[1]
    slab_len = potential.shape[0] * groups
    sticks = stick_list.shape[0]
    columns = stick_list.T
    fwd, transposed = plane_tables(box_edge, grid_len)
    z_inverse, z_forward = z_tables(box_edge, slab_len, grid_len)
    in_hbm = functools.partial(pltpu.with_memory_space_constraint, memory_space=pltpu.HBM)
    hbm, vmem = pl.BlockSpec(memory_space=pltpu.HBM), pl.BlockSpec(memory_space=pltpu.VMEM)
    mates = 2 if bands % 2 == 0 else 1
    count = bands // mates

    send, *operands = pl.pallas_call(
        functools.partial(head_kernel, count),
        out_shape=[
            jax.ShapeDtypeStruct((count * groups, 2, stick_dev), F32),
            jax.ShapeDtypeStruct((box_edge, sticks), BF16),
            jax.ShapeDtypeStruct((box_edge, sticks), BF16),
            jax.ShapeDtypeStruct((grid_len, grid_len), BF16),
            jax.ShapeDtypeStruct((2, box_edge, grid_len), BF16),
            jax.ShapeDtypeStruct((2, grid_len, box_edge), BF16),
        ],
        in_specs=[hbm] * 6,
        out_specs=[vmem] * 6,
        scratch_shapes=[
            pltpu.VMEM((2, stick_dev, box_edge), BF16),
            pltpu.VMEM((2, sticks), jnp.int32),
            pltpu.VMEM(z_inverse.shape, BF16),
            pltpu.SemaphoreType.DMA((6,)),
        ],
        compiler_params=pltpu.CompilerParams(vmem_limit_bytes=8 << 20),
        name="head",
    )(
        in_hbm(band_coeffs[0]),
        in_hbm(columns),
        in_hbm(z_inverse),
        in_hbm(potential[0]),
        in_hbm(fwd),
        in_hbm(transposed),
    )
    first = [
        [
            (q * mates + (side + q) % mates) * groups + g
            for g in sorted(range(groups), key=lambda g: first_place(g, groups))
            for q in [(lead_pair(side, mates) + t) % count for t in range(count)]
        ]
        for side in range(mates)
    ]
    second = sorted(
        ((g, b) for g in range(groups) for b in range(mates)), key=lambda member: place_of(*member, groups, mates)
    )
    second = [[(q * mates + b) * groups + g for g, b in second] for q in range(count)]
    planes = lax.all_to_all(
        send, ("band", "pw"), split_axis=0, concat_axis=0, tiled=True, axis_index_groups=first
    )
    others = [
        lax.ppermute(planes, "band", [(b, b - b % mates + (b + s) % mates) for b in range(bands)])
        for s in range(1, mates)
    ]
    span = -(-bands // 8) * 8
    rows, zeds = pl.pallas_call(
        functools.partial(plane_kernel, mates, count),
        out_shape=[
            jax.ShapeDtypeStruct((2, sticks), F32),
            jax.ShapeDtypeStruct((span, 2 * sticks), F32),
        ],
        in_specs=[vmem] * 6,
        out_specs=[vmem] * 2,
        scratch_shapes=[
            pltpu.VMEM((2 * box_edge, sticks), BF16),
            pltpu.VMEM((2, box_edge, grid_len), BF16),
            pltpu.VMEM((4, grid_len // 2, grid_len), F32),
            pltpu.VMEM((2, 2, grid_len // 2, grid_len), BF16),
            pltpu.VMEM((2, grid_len, box_edge), BF16),
            pltpu.VMEM((2 * box_edge, box_edge), BF16),
        ],
        compiler_params=pltpu.CompilerParams(vmem_limit_bytes=16 << 20),
        cost_estimate=pl.CostEstimate(flops=1_400_000_000, bytes_accessed=3 << 20, transcendentals=0),
        name="plane",
    )(planes, *operands)
    backs = pl.pallas_call(
        functools.partial(pair_kernel, mates, count),
        out_shape=jax.ShapeDtypeStruct((mates * groups, 4, stick_dev), F32),
        in_specs=[vmem] * (1 + mates),
        out_specs=vmem,
        scratch_shapes=[pltpu.VMEM((span, 2 * sticks), F32)],
        compiler_params=pltpu.CompilerParams(vmem_limit_bytes=4 << 20),
        name="pairs",
    )(zeds, rows, *others)
    back = lax.all_to_all(
        backs,
        ("band", "pw"),
        split_axis=0,
        concat_axis=0,
        tiled=True,
        axis_index_groups=second,
    )
    applied, correlation = pl.pallas_call(
        functools.partial(tail_kernel, mates, 1.0 / math.sqrt(slab_len * sticks)),
        out_shape=[
            jax.ShapeDtypeStruct((2, stick_dev, box_edge), BF16),
            jax.ShapeDtypeStruct((2, 1, bands), F32),
        ],
        in_specs=[vmem] * 3,
        out_specs=[hbm] * 2,
        scratch_shapes=[
            pltpu.VMEM((2, stick_dev, box_edge), BF16),
            pltpu.VMEM((2, 1, bands), F32),
            pltpu.SemaphoreType.DMA((3,)),
        ],
        compiler_params=pltpu.CompilerParams(vmem_limit_bytes=4 << 20),
        name="tail",
    )(back, columns, z_forward)
    return applied[None], correlation.transpose(0, 2, 1)


def solution(mesh):
    return jax.shard_map(
        local,
        mesh=mesh,
        in_specs=(P("band", None, "pw", None), P("pw", None, None), P()),
        out_specs=(P("band", None, "pw", None), P(None, None, "band")),
        check_vma=False,
    )
```

```python
import functools
import math

import jax
import jax.numpy as jnp
import numpy as np
from jax import lax
from jax.experimental import pallas as pl
from jax.experimental.pallas import tpu as pltpu
from jax.sharding import PartitionSpec as P

F32 = jnp.float32
BF16 = jnp.bfloat16


def first_place(group, groups):
    return ((groups - 3) - group) % groups


def place_of(group, mate, groups, mates):
    return (groups - 1 - group) % groups * mates + mates - 1 - mate


def side_of(mates):
    band = lax.axis_index("band")
    return lax.rem(lax.rem(band, mates) + (mates - 1) * (band // mates), mates)


def lead_pair(side, mates):
    return side % mates


def phases(box_index, grid_index, period, factor):
    turns = box_index[:, None] * grid_index[None, :] % period
    angles = turns * (2.0 * math.pi / period)
    return np.cos(angles) * factor, np.sin(angles) * factor


def plane_tables(box_edge, grid_len):
    half = grid_len // 2
    mats = []
    for parity in range(2):
        cos, sin = phases(
            np.arange(parity, box_edge, 2) - box_edge // 2, np.arange(half), grid_len, 1.0 / math.sqrt(box_edge)
        )
        mats.append(np.block([[cos, sin], [-sin, cos]]))
    mats = np.stack(mats)
    return jnp.asarray(mats[:, : box_edge // 2], BF16), jnp.asarray(mats.transpose(0, 2, 1)[:, :half], BF16)


def z_tables(box_edge, slab_len, grid_len):
    cos, sin = phases(np.arange(box_edge) - box_edge // 2, np.arange(slab_len), grid_len, 1.0)
    inverse = np.stack([np.concatenate([cos.T, -sin.T], 1), np.concatenate([sin.T, cos.T], 1)], 1)
    inverse = inverse.reshape(2 * slab_len, 2 * box_edge) / math.sqrt(box_edge)
    forward = np.block([[cos.T, -sin.T], [sin.T, cos.T]]) / math.sqrt(slab_len)
    return jnp.asarray(inverse, BF16), jnp.asarray(forward, BF16)


def dot_nt(left, right):
    return lax.dot_general(left, right, (((1,), (1,)), ((), ())), preferred_element_type=F32)


def dot_tn(left, right):
    return lax.dot_general(left, right, (((0,), (0,)), ((), ())), preferred_element_type=F32)


def dot_nn(left, right):
    return jnp.dot(left, right, preferred_element_type=F32)


def own_sphere(sticks_ref, stick_dev, box_edge):
    middle = box_edge // 2
    start = pl.multiple_of(lax.axis_index("pw") * stick_dev, stick_dev)
    own = sticks_ref[:, pl.ds(start, stick_dev)] - middle
    own = (own * own).astype(F32)
    radial = own[0:1] + own[1:2]
    column = jnp.broadcast_to(radial, (8, stick_dev)).T[:, 0:1]
    level = lax.broadcasted_iota(jnp.int32, (1, box_edge), 1) - middle
    return column + (level * level).astype(F32) < float(middle * middle)


def head_kernel(
    count,
    coeffs_hbm,
    sticks_hbm,
    table_hbm,
    pot_hbm,
    fwd_hbm,
    tr_hbm,
    out_ref,
    hot_a,
    hot_b,
    pot_ref,
    fwd_ref,
    tr_ref,
    coeffs_ref,
    sticks_ref,
    table_ref,
    sems,
):
    side, n_half = fwd_hbm.shape[1], tr_hbm.shape[1]
    pairs = [
        (sticks_hbm, sticks_ref),
        (coeffs_hbm, coeffs_ref),
        (table_hbm, table_ref),
        (fwd_hbm, fwd_ref.at[:, :side]),
        (tr_hbm, tr_ref.at[:, :n_half]),
        (pot_hbm, pot_ref),
    ]
    copies = [pltpu.make_async_copy(src, dst, sems.at[n]) for n, (src, dst) in enumerate(pairs)]
    for n, copy in enumerate(copies):
        copy.start(priority=n // 3)
    _, stick_dev, box_edge = coeffs_ref.shape
    slab_len = table_ref.shape[0] // 2
    copies[0].wait()
    sphere = own_sphere(sticks_ref, stick_dev, box_edge)
    copies[1].wait()
    copies[2].wait()
    masked = [jnp.where(sphere, coeffs_ref[c].astype(F32), 0.0).astype(BF16) for c in range(2)]
    masked = jnp.concatenate(masked, axis=1)
    rows = dot_nt(table_ref[...], masked).astype(BF16).astype(F32)
    for z in range(slab_len):
        for t in range(count):
            out_ref[first_place(z, slab_len) * count + t] = rows[2 * z : 2 * z + 2]

    codes = sticks_ref[...]
    codes = ((codes & 1) * side + (codes >> 1)).astype(F32).astype(BF16)
    rows = lax.broadcasted_iota(jnp.int32, (box_edge, stick_dev), 0).astype(F32).astype(BF16)
    one, none = jnp.ones((), BF16), jnp.zeros((), BF16)
    for at in range(0, codes.shape[1], stick_dev):
        cols = slice(at, at + stick_dev)
        hot_a[:, cols] = jnp.where(rows == codes[0:1, cols], one, none)
        hot_b[:, cols] = jnp.where(rows == codes[1:2, cols], one, none)
    for copy in copies[3:5]:
        copy.wait()
    for p in range(2):
        fwd_ref[p, side:, :n_half] = -fwd_ref[p, :side, n_half:]
        fwd_ref[p, side:, n_half:] = fwd_ref[p, :side, :n_half]
        tr_ref[p, n_half:, :side] = -tr_ref[p, :n_half, side:]
        tr_ref[p, n_half:, side:] = tr_ref[p, :n_half, :side]
    copies[5].wait()


def plane_kernel(
    mates,
    count,
    recv_ref,
    hot_a,
    hot_b,
    pot_ref,
    fwd_ref,
    tr_ref,
    back_ref,
    zeds_ref,
    spread,
    half_ref,
    wide_ref,
    left_ref,
    mid_ref,
    cell_ref,
):
    box_edge, sticks = hot_a.shape
    side = box_edge // 2
    groups = recv_ref.shape[0] // count
    per = sticks // groups
    grid_len = pot_ref.shape[0]
    n_half = grid_len // 2

    own_place = lax.rem(lax.axis_index("band") // mates - lead_pair(side_of(mates), mates) + count, count)
    for g in range(groups):
        cols = slice(g * per, (g + 1) * per)
        own = recv_ref[first_place(g, groups) * count + own_place].astype(BF16)
        for c in range(2):
            placed = hot_b[:, cols] * own[c : c + 1]
            for p in range(2):
                row = p * box_edge + c * side
                spread[row : row + side, cols] = placed[p * side : (p + 1) * side]

    box = dot_nt(hot_a[...], spread[...]).astype(BF16)
    for p in range(2):
        wide_ref[p] = dot_nn(box[:, p * box_edge : (p + 1) * box_edge], fwd_ref[p])
    for r in range(0, box_edge, 16):
        even, odd = wide_ref[0, r : r + 16], wide_ref[1, r : r + 16]
        p, at = r // side, r % side
        for n, both in enumerate((even + odd, even - odd)):
            both = both.astype(BF16)
            for c in range(2):
                half_ref[p, c * side + at : c * side + at + 16, n * n_half : (n + 1) * n_half] = both[
                    :, c * n_half : (c + 1) * n_half
                ]

    for c in range(2):
        for p in range(2):
            wide_ref[2 * c + p] = dot_nn(tr_ref[p, c * n_half : (c + 1) * n_half], half_ref[p])
    for r in range(0, n_half, 16):
        rows = slice(r, r + 16)
        pot_near = pot_ref[rows].astype(F32)
        pot_far = pot_ref[n_half + r : n_half + r + 16].astype(F32)
        for c in range(2):
            cols = slice(c * n_half, (c + 1) * n_half)
            even, odd = wide_ref[2 * c, rows], wide_ref[2 * c + 1, rows]
            near = (even + odd) * pot_near
            far = (even - odd) * pot_far
            for p, both in ((0, near + far), (1, near - far)):
                left_ref[p, 0, rows, cols] = (both[:, :n_half] + both[:, n_half:]).astype(BF16)
                left_ref[p, 1, rows, cols] = (both[:, :n_half] - both[:, n_half:]).astype(BF16)
    for p in range(2):
        for q in range(2):
            mid = dot_nn(left_ref[p, q], tr_ref[q]).astype(BF16)
            for c in range(2):
                mid_ref[p, c * n_half : (c + 1) * n_half, q * side : (q + 1) * side] = mid[
                    :, c * side : (c + 1) * side
                ]

    for p in range(2):
        cell_ref[p * box_edge : (p + 1) * box_edge] = dot_nn(fwd_ref[p], mid_ref[p]).astype(BF16)

    wide = 256
    for s0 in range(0, sticks, wide):
        cols = slice(s0, s0 + wide)
        picked = dot_nn(cell_ref[...], hot_b[:, cols])
        parts = [None, None]
        for p in range(2):
            for r in range(0, side, 16):
                hot = hot_a[p * side + r : p * side + r + 16, cols].astype(F32)
                for c in range(2):
                    at = p * box_edge + c * side + r
                    term = picked[at : at + 16] * hot
                    term = term[:8] + term[8:]
                    parts[c] = term if parts[c] is None else parts[c] + term
        parts = [jnp.sum(part, axis=0, keepdims=True) for part in parts]
        back = jnp.concatenate(parts, axis=0) * (float(box_edge) / float(grid_len))
        back_ref[:, cols] = back.astype(BF16).astype(F32)
    zeds_ref[...] = jnp.zeros_like(zeds_ref)
    gather_rows(count, 0, recv_ref, zeds_ref)


def gather_rows(count, shift, recv_ref, rows_ref):
    groups, per = recv_ref.shape[0] // count, recv_ref.shape[2]
    for t in range(count):
        row = shift * count + t
        for g in range(groups):
            block = recv_ref[first_place(g, groups) * count + t]
            for c in range(2):
                at = (c * groups + g) * per
                rows_ref[row : row + 1, at : at + per] = block[c : c + 1]


def pair_kernel(mates, count, seen_ref, back_ref, *refs):
    others, out_ref, zeds_ref = refs[: mates - 1], refs[mates - 1], refs[mates]
    zeds_ref[...] = seen_ref[...]
    for s in range(1, mates):
        gather_rows(count, s, others[s - 1], zeds_ref)
    back = back_ref[...].astype(BF16)
    left = jnp.concatenate(
        [jnp.concatenate([back[0:1], back[1:2]], axis=1), jnp.concatenate([back[1:2], -back[0:1]], axis=1)], axis=0
    )
    total = dot_nt(left, zeds_ref[...].astype(BF16))
    bands = mates * count
    blocks, _, per = out_ref.shape
    groups = blocks // mates
    for g in range(groups):
        for b in range(mates):
            at = place_of(g, b, groups, mates)
            out_ref[at, 0:2] = back_ref[:, g * per : (g + 1) * per]
            out_ref[at, 2:4, :bands] = total[:, :bands]
            out_ref[at, 2:4, bands:] = jnp.zeros((2, per - bands), F32)


def tail_kernel(mates, scale, recv_ref, sticks_ref, table_ref, out_hbm, corr_hbm, out_ref, corr_ref, sems):
    blocks, _, stick_dev = recv_ref.shape
    groups = blocks // mates
    own_mate = lax.rem(lax.axis_index("band"), mates)
    box_edge = out_ref.shape[2]
    own = [recv_ref[place_of(g, own_mate, groups, mates)] for g in range(groups)]
    total = own[0][2:4]
    for part in own[1:]:
        total = total + part[2:4]
    total = total * scale
    side = side_of(mates)
    count = corr_ref.shape[2] // mates
    for q in range(count):
        for b in range(mates):
            group, at = (b - q) % mates, q * mates + b
            column = None
            for k in range(mates):
                row = (k - group) % mates * count + (q - lead_pair(group, mates)) % count
                here = total[:, row : row + 1]
                column = here if column is None else jnp.where(side == k, here, column)
            for c in range(2):
                corr_ref[c, :, at : at + 1] = column[c : c + 1]
    corr_copy = pltpu.make_async_copy(corr_ref, corr_hbm, sems.at[2])
    corr_copy.start(priority=1)
    sphere = own_sphere(sticks_ref, stick_dev, box_edge)
    back = jnp.concatenate([part[c : c + 1] for c in range(2) for part in own], axis=0).astype(BF16)
    copies = []
    for c in range(2):
        values = dot_tn(back, table_ref[:, c * box_edge : (c + 1) * box_edge])
        out_ref[c] = jnp.where(sphere, values, 0.0).astype(BF16)
        copies.append(pltpu.make_async_copy(out_ref.at[c], out_hbm.at[c], sems.at[c]))
        copies[-1].start(priority=c)
    for copy in copies:
        copy.wait()
    corr_copy.wait()


def local(band_coeffs, potential, stick_list):
    groups = lax.axis_size("pw")
    bands = lax.axis_size("band")
    _, _, stick_dev, box_edge = band_coeffs.shape
    grid_len = potential.shape[1]
    slab_len = potential.shape[0] * groups
    sticks = stick_list.shape[0]
    columns = stick_list.T
    fwd, transposed = plane_tables(box_edge, grid_len)
    z_inverse, z_forward = z_tables(box_edge, slab_len, grid_len)
    in_hbm = functools.partial(pltpu.with_memory_space_constraint, memory_space=pltpu.HBM)
    hbm, vmem = pl.BlockSpec(memory_space=pltpu.HBM), pl.BlockSpec(memory_space=pltpu.VMEM)
    mates = 2 if bands % 2 == 0 else 1
    count = bands // mates

    send, *operands = pl.pallas_call(
        functools.partial(head_kernel, count),
        out_shape=[
            jax.ShapeDtypeStruct((count * groups, 2, stick_dev), F32),
            jax.ShapeDtypeStruct((box_edge, sticks), BF16),
            jax.ShapeDtypeStruct((box_edge, sticks), BF16),
            jax.ShapeDtypeStruct((grid_len, grid_len), BF16),
            jax.ShapeDtypeStruct((2, box_edge, grid_len), BF16),
            jax.ShapeDtypeStruct((2, grid_len, box_edge), BF16),
        ],
        in_specs=[hbm] * 6,
        out_specs=[vmem] * 6,
        scratch_shapes=[
            pltpu.VMEM((2, stick_dev, box_edge), BF16),
            pltpu.VMEM((2, sticks), jnp.int32),
            pltpu.VMEM(z_inverse.shape, BF16),
            pltpu.SemaphoreType.DMA((6,)),
        ],
        compiler_params=pltpu.CompilerParams(vmem_limit_bytes=8 << 20),
        name="head",
    )(
        in_hbm(band_coeffs[0]),
        in_hbm(columns),
        in_hbm(z_inverse),
        in_hbm(potential[0]),
        in_hbm(fwd),
        in_hbm(transposed),
    )
    first = [
        [
            (q * mates + (side + q) % mates) * groups + g
            for g in sorted(range(groups), key=lambda g: first_place(g, groups))
            for q in [(lead_pair(side, mates) + t) % count for t in range(count)]
        ]
        for side in range(mates)
    ]
    second = sorted(
        ((g, b) for g in range(groups) for b in range(mates)), key=lambda member: place_of(*member, groups, mates)
    )
    second = [[(q * mates + b) * groups + g for g, b in second] for q in range(count)]
    planes = lax.all_to_all(
        send, ("band", "pw"), split_axis=0, concat_axis=0, tiled=True, axis_index_groups=first
    )
    others = [
        lax.ppermute(planes, "band", [(b, b - b % mates + (b + s) % mates) for b in range(bands)])
        for s in range(1, mates)
    ]
    span = -(-bands // 8) * 8
    rows, zeds = pl.pallas_call(
        functools.partial(plane_kernel, mates, count),
        out_shape=[
            jax.ShapeDtypeStruct((2, sticks), F32),
            jax.ShapeDtypeStruct((span, 2 * sticks), F32),
        ],
        in_specs=[vmem] * 6,
        out_specs=[vmem] * 2,
        scratch_shapes=[
            pltpu.VMEM((2 * box_edge, sticks), BF16),
            pltpu.VMEM((2, box_edge, grid_len), BF16),
            pltpu.VMEM((4, grid_len // 2, grid_len), F32),
            pltpu.VMEM((2, 2, grid_len // 2, grid_len), BF16),
            pltpu.VMEM((2, grid_len, box_edge), BF16),
            pltpu.VMEM((2 * box_edge, box_edge), BF16),
        ],
        compiler_params=pltpu.CompilerParams(vmem_limit_bytes=16 << 20),
        cost_estimate=pl.CostEstimate(flops=1_400_000_000, bytes_accessed=3 << 20, transcendentals=0),
        name="plane",
    )(planes, *operands)
    backs = pl.pallas_call(
        functools.partial(pair_kernel, mates, count),
        out_shape=jax.ShapeDtypeStruct((mates * groups, 4, stick_dev), F32),
        in_specs=[vmem] * (1 + mates),
        out_specs=vmem,
        scratch_shapes=[pltpu.VMEM((span, 2 * sticks), F32)],
        compiler_params=pltpu.CompilerParams(vmem_limit_bytes=4 << 20),
        name="pairs",
    )(zeds, rows, *others)
    back = lax.all_to_all(
        backs,
        ("band", "pw"),
        split_axis=0,
        concat_axis=0,
        tiled=True,
        axis_index_groups=second,
    )
    applied, correlation = pl.pallas_call(
        functools.partial(tail_kernel, mates, 1.0 / math.sqrt(slab_len * sticks)),
        out_shape=[
            jax.ShapeDtypeStruct((2, stick_dev, box_edge), BF16),
            jax.ShapeDtypeStruct((2, 1, bands), F32),
        ],
        in_specs=[vmem] * 3,
        out_specs=[hbm] * 2,
        scratch_shapes=[
            pltpu.VMEM((2, stick_dev, box_edge), BF16),
            pltpu.VMEM((2, 1, bands), F32),
            pltpu.SemaphoreType.DMA((3,)),
        ],
        compiler_params=pltpu.CompilerParams(vmem_limit_bytes=4 << 20),
        name="tail",
    )(back, columns, z_forward)
    return applied[None], correlation.transpose(0, 2, 1)


def solution(mesh):
    return jax.shard_map(
        local,
        mesh=mesh,
        in_specs=(P("band", None, "pw", None), P("pw", None, None), P()),
        out_specs=(P("band", None, "pw", None), P(None, None, "band")),
        check_vma=False,
    )
```

```python
import functools
import math

import jax
import jax.numpy as jnp
import numpy as np
from jax import lax
from jax.experimental import pallas as pl
from jax.experimental.pallas import tpu as pltpu
from jax.sharding import PartitionSpec as P

F32 = jnp.float32
BF16 = jnp.bfloat16


def first_place(group, groups):
    return ((groups - 3) - group) % groups


def place_of(group, mate, groups, mates):
    return (groups - 1 - group) % groups * mates + mates - 1 - mate


def side_of(mates):
    band = lax.axis_index("band")
    return lax.rem(lax.rem(band, mates) + (mates - 1) * (band // mates), mates)


def lead_pair(side, mates):
    return side % mates


def phases(box_index, grid_index, period, factor):
    turns = box_index[:, None] * grid_index[None, :] % period
    angles = turns * (2.0 * math.pi / period)
    return np.cos(angles) * factor, np.sin(angles) * factor


def plane_tables(box_edge, grid_len):
    half = grid_len // 2
    mats = []
    for parity in range(2):
        cos, sin = phases(
            np.arange(parity, box_edge, 2) - box_edge // 2, np.arange(half), grid_len, 1.0 / math.sqrt(box_edge)
        )
        mats.append(np.block([[cos, sin], [-sin, cos]]))
    mats = np.stack(mats)
    return jnp.asarray(mats[:, : box_edge // 2], BF16), jnp.asarray(mats.transpose(0, 2, 1)[:, :half], BF16)


def z_tables(box_edge, slab_len, grid_len):
    cos, sin = phases(np.arange(box_edge) - box_edge // 2, np.arange(slab_len), grid_len, 1.0)
    inverse = np.stack([np.concatenate([cos.T, -sin.T], 1), np.concatenate([sin.T, cos.T], 1)], 1)
    inverse = inverse.reshape(2 * slab_len, 2 * box_edge) / math.sqrt(box_edge)
    forward = np.block([[cos.T, -sin.T], [sin.T, cos.T]]) / math.sqrt(slab_len)
    return jnp.asarray(inverse, BF16), jnp.asarray(forward, BF16)


def dot_nt(left, right):
    return lax.dot_general(left, right, (((1,), (1,)), ((), ())), preferred_element_type=F32)


def dot_tn(left, right):
    return lax.dot_general(left, right, (((0,), (0,)), ((), ())), preferred_element_type=F32)


def dot_nn(left, right):
    return jnp.dot(left, right, preferred_element_type=F32)


def own_sphere(sticks_ref, stick_dev, box_edge):
    middle = box_edge // 2
    start = pl.multiple_of(lax.axis_index("pw") * stick_dev, stick_dev)
    own = sticks_ref[:, pl.ds(start, stick_dev)] - middle
    own = (own * own).astype(F32)
    radial = own[0:1] + own[1:2]
    column = jnp.broadcast_to(radial, (8, stick_dev)).T[:, 0:1]
    level = lax.broadcasted_iota(jnp.int32, (1, box_edge), 1) - middle
    return column + (level * level).astype(F32) < float(middle * middle)


def head_kernel(
    count,
    coeffs_hbm,
    sticks_hbm,
    table_hbm,
    pot_hbm,
    fwd_hbm,
    tr_hbm,
    out_ref,
    hot_a,
    hot_b,
    pot_ref,
    fwd_ref,
    tr_ref,
    coeffs_ref,
    sticks_ref,
    table_ref,
    sems,
):
    side, n_half = fwd_hbm.shape[1], tr_hbm.shape[1]
    pairs = [
        (sticks_hbm, sticks_ref),
        (table_hbm, table_ref),
        (coeffs_hbm, coeffs_ref),
        (fwd_hbm, fwd_ref.at[:, :side]),
        (tr_hbm, tr_ref.at[:, :n_half]),
        (pot_hbm, pot_ref),
    ]
    copies = [pltpu.make_async_copy(src, dst, sems.at[n]) for n, (src, dst) in enumerate(pairs)]
    for n, copy in enumerate(copies):
        copy.start(priority=int(n not in (0, 2)))
    _, stick_dev, box_edge = coeffs_ref.shape
    slab_len = table_ref.shape[0] // 2
    copies[0].wait()
    sphere = own_sphere(sticks_ref, stick_dev, box_edge)
    copies[2].wait()
    copies[1].wait()
    masked = [jnp.where(sphere, coeffs_ref[c].astype(F32), 0.0).astype(BF16) for c in range(2)]
    masked = jnp.concatenate(masked, axis=1)
    rows = dot_nt(table_ref[...], masked).astype(BF16).astype(F32)
    for z in range(slab_len):
        for t in range(count):
            out_ref[first_place(z, slab_len) * count + t] = rows[2 * z : 2 * z + 2]

    codes = sticks_ref[...]
    codes = ((codes & 1) * side + (codes >> 1)).astype(F32).astype(BF16)
    rows = lax.broadcasted_iota(jnp.int32, (box_edge, stick_dev), 0).astype(F32).astype(BF16)
    one, none = jnp.ones((), BF16), jnp.zeros((), BF16)
    for at in range(0, codes.shape[1], stick_dev):
        cols = slice(at, at + stick_dev)
        hot_a[:, cols] = jnp.where(rows == codes[0:1, cols], one, none)
        hot_b[:, cols] = jnp.where(rows == codes[1:2, cols], one, none)
    for copy in copies[3:5]:
        copy.wait()
    for p in range(2):
        fwd_ref[p, side:, :n_half] = -fwd_ref[p, :side, n_half:]
        fwd_ref[p, side:, n_half:] = fwd_ref[p, :side, :n_half]
        tr_ref[p, n_half:, :side] = -tr_ref[p, :n_half, side:]
        tr_ref[p, n_half:, side:] = tr_ref[p, :n_half, :side]
    copies[5].wait()


def plane_kernel(
    mates,
    count,
    recv_ref,
    hot_a,
    hot_b,
    pot_ref,
    fwd_ref,
    tr_ref,
    back_ref,
    zeds_ref,
    spread,
    half_ref,
    wide_ref,
    left_ref,
    mid_ref,
    cell_ref,
):
    box_edge, sticks = hot_a.shape
    side = box_edge // 2
    groups = recv_ref.shape[0] // count
    per = sticks // groups
    grid_len = pot_ref.shape[0]
    n_half = grid_len // 2

    own_place = lax.rem(lax.axis_index("band") // mates - lead_pair(side_of(mates), mates) + count, count)
    for g in range(groups):
        cols = slice(g * per, (g + 1) * per)
        own = recv_ref[first_place(g, groups) * count + own_place].astype(BF16)
        for c in range(2):
            placed = hot_b[:, cols] * own[c : c + 1]
            for p in range(2):
                row = p * box_edge + c * side
                spread[row : row + side, cols] = placed[p * side : (p + 1) * side]

    box = dot_nt(hot_a[...], spread[...]).astype(BF16)
    for p in range(2):
        wide_ref[p] = dot_nn(box[:, p * box_edge : (p + 1) * box_edge], fwd_ref[p])
    for r in range(0, box_edge, 16):
        even, odd = wide_ref[0, r : r + 16], wide_ref[1, r : r + 16]
        p, at = r // side, r % side
        for n, both in enumerate((even + odd, even - odd)):
            both = both.astype(BF16)
            for c in range(2):
                half_ref[p, c * side + at : c * side + at + 16, n * n_half : (n + 1) * n_half] = both[
                    :, c * n_half : (c + 1) * n_half
                ]

    for c in range(2):
        for p in range(2):
            wide_ref[2 * c + p] = dot_nn(tr_ref[p, c * n_half : (c + 1) * n_half], half_ref[p])
    for r in range(0, n_half, 16):
        rows = slice(r, r + 16)
        pot_near = pot_ref[rows].astype(F32)
        pot_far = pot_ref[n_half + r : n_half + r + 16].astype(F32)
        for c in range(2):
            cols = slice(c * n_half, (c + 1) * n_half)
            even, odd = wide_ref[2 * c, rows], wide_ref[2 * c + 1, rows]
            near = (even + odd) * pot_near
            far = (even - odd) * pot_far
            for p, both in ((0, near + far), (1, near - far)):
                left_ref[p, 0, rows, cols] = (both[:, :n_half] + both[:, n_half:]).astype(BF16)
                left_ref[p, 1, rows, cols] = (both[:, :n_half] - both[:, n_half:]).astype(BF16)
    for p in range(2):
        for q in range(2):
            mid = dot_nn(left_ref[p, q], tr_ref[q]).astype(BF16)
            for c in range(2):
                mid_ref[p, c * n_half : (c + 1) * n_half, q * side : (q + 1) * side] = mid[
                    :, c * side : (c + 1) * side
                ]

    for p in range(2):
        cell_ref[p * box_edge : (p + 1) * box_edge] = dot_nn(fwd_ref[p], mid_ref[p]).astype(BF16)

    wide = 256
    for s0 in range(0, sticks, wide):
        cols = slice(s0, s0 + wide)
        picked = dot_nn(cell_ref[...], hot_b[:, cols])
        parts = [None, None]
        for p in range(2):
            for r in range(0, side, 16):
                hot = hot_a[p * side + r : p * side + r + 16, cols].astype(F32)
                for c in range(2):
                    at = p * box_edge + c * side + r
                    term = picked[at : at + 16] * hot
                    term = term[:8] + term[8:]
                    parts[c] = term if parts[c] is None else parts[c] + term
        parts = [jnp.sum(part, axis=0, keepdims=True) for part in parts]
        back = jnp.concatenate(parts, axis=0) * (float(box_edge) / float(grid_len))
        back_ref[:, cols] = back.astype(BF16).astype(F32)
    zeds_ref[...] = jnp.zeros_like(zeds_ref)
    gather_rows(count, 0, recv_ref, zeds_ref)


def gather_rows(count, shift, recv_ref, rows_ref):
    groups, per = recv_ref.shape[0] // count, recv_ref.shape[2]
    for t in range(count):
        row = shift * count + t
        for g in range(groups):
            block = recv_ref[first_place(g, groups) * count + t]
            for c in range(2):
                at = (c * groups + g) * per
                rows_ref[row : row + 1, at : at + per] = block[c : c + 1]


def pair_kernel(mates, count, seen_ref, back_ref, *refs):
    others, out_ref, zeds_ref = refs[: mates - 1], refs[mates - 1], refs[mates]
    zeds_ref[...] = seen_ref[...]
    for s in range(1, mates):
        gather_rows(count, s, others[s - 1], zeds_ref)
    back = back_ref[...].astype(BF16)
    left = jnp.concatenate(
        [jnp.concatenate([back[0:1], back[1:2]], axis=1), jnp.concatenate([back[1:2], -back[0:1]], axis=1)], axis=0
    )
    total = dot_nt(left, zeds_ref[...].astype(BF16))
    bands = mates * count
    blocks, _, per = out_ref.shape
    groups = blocks // mates
    for g in range(groups):
        for b in range(mates):
            at = place_of(g, b, groups, mates)
            out_ref[at, 0:2] = back_ref[:, g * per : (g + 1) * per]
            out_ref[at, 2:4, :bands] = total[:, :bands]
            out_ref[at, 2:4, bands:] = jnp.zeros((2, per - bands), F32)


def tail_kernel(mates, scale, recv_ref, sticks_ref, table_ref, out_hbm, corr_hbm, out_ref, corr_ref, sems):
    blocks, _, stick_dev = recv_ref.shape
    groups = blocks // mates
    own_mate = lax.rem(lax.axis_index("band"), mates)
    box_edge = out_ref.shape[2]
    own = [recv_ref[place_of(g, own_mate, groups, mates)] for g in range(groups)]
    total = own[0][2:4]
    for part in own[1:]:
        total = total + part[2:4]
    total = total * scale
    side = side_of(mates)
    count = corr_ref.shape[2] // mates
    for q in range(count):
        for b in range(mates):
            group, at = (b - q) % mates, q * mates + b
            column = None
            for k in range(mates):
                row = (k - group) % mates * count + (q - lead_pair(group, mates)) % count
                here = total[:, row : row + 1]
                column = here if column is None else jnp.where(side == k, here, column)
            for c in range(2):
                corr_ref[c, :, at : at + 1] = column[c : c + 1]
    corr_copy = pltpu.make_async_copy(corr_ref, corr_hbm, sems.at[2])
    corr_copy.start(priority=1)
    sphere = own_sphere(sticks_ref, stick_dev, box_edge)
    back = jnp.concatenate([part[c : c + 1] for c in range(2) for part in own], axis=0).astype(BF16)
    copies = []
    for c in range(2):
        values = dot_tn(back, table_ref[:, c * box_edge : (c + 1) * box_edge])
        out_ref[c] = jnp.where(sphere, values, 0.0).astype(BF16)
        copies.append(pltpu.make_async_copy(out_ref.at[c], out_hbm.at[c], sems.at[c]))
        copies[-1].start(priority=c)
    for copy in copies:
        copy.wait()
    corr_copy.wait()


def local(band_coeffs, potential, stick_list):
    groups = lax.axis_size("pw")
    bands = lax.axis_size("band")
    _, _, stick_dev, box_edge = band_coeffs.shape
    grid_len = potential.shape[1]
    slab_len = potential.shape[0] * groups
    sticks = stick_list.shape[0]
    columns = stick_list.T
    fwd, transposed = plane_tables(box_edge, grid_len)
    z_inverse, z_forward = z_tables(box_edge, slab_len, grid_len)
    in_hbm = functools.partial(pltpu.with_memory_space_constraint, memory_space=pltpu.HBM)
    hbm, vmem = pl.BlockSpec(memory_space=pltpu.HBM), pl.BlockSpec(memory_space=pltpu.VMEM)
    mates = 2 if bands % 2 == 0 else 1
    count = bands // mates

    send, *operands = pl.pallas_call(
        functools.partial(head_kernel, count),
        out_shape=[
            jax.ShapeDtypeStruct((count * groups, 2, stick_dev), F32),
            jax.ShapeDtypeStruct((box_edge, sticks), BF16),
            jax.ShapeDtypeStruct((box_edge, sticks), BF16),
            jax.ShapeDtypeStruct((grid_len, grid_len), BF16),
            jax.ShapeDtypeStruct((2, box_edge, grid_len), BF16),
            jax.ShapeDtypeStruct((2, grid_len, box_edge), BF16),
        ],
        in_specs=[hbm] * 6,
        out_specs=[vmem] * 6,
        scratch_shapes=[
            pltpu.VMEM((2, stick_dev, box_edge), BF16),
            pltpu.VMEM((2, sticks), jnp.int32),
            pltpu.VMEM(z_inverse.shape, BF16),
            pltpu.SemaphoreType.DMA((6,)),
        ],
        compiler_params=pltpu.CompilerParams(vmem_limit_bytes=8 << 20),
        name="head",
    )(
        in_hbm(band_coeffs[0]),
        in_hbm(columns),
        in_hbm(z_inverse),
        in_hbm(potential[0]),
        in_hbm(fwd),
        in_hbm(transposed),
    )
    first = [
        [
            (q * mates + (side + q) % mates) * groups + g
            for g in sorted(range(groups), key=lambda g: first_place(g, groups))
            for q in [(lead_pair(side, mates) + t) % count for t in range(count)]
        ]
        for side in range(mates)
    ]
    second = sorted(
        ((g, b) for g in range(groups) for b in range(mates)), key=lambda member: place_of(*member, groups, mates)
    )
    second = [[(q * mates + b) * groups + g for g, b in second] for q in range(count)]
    planes = lax.all_to_all(
        send, ("band", "pw"), split_axis=0, concat_axis=0, tiled=True, axis_index_groups=first
    )
    others = [
        lax.ppermute(planes, "band", [(b, b - b % mates + (b + s) % mates) for b in range(bands)])
        for s in range(1, mates)
    ]
    span = -(-bands // 8) * 8
    rows, zeds = pl.pallas_call(
        functools.partial(plane_kernel, mates, count),
        out_shape=[
            jax.ShapeDtypeStruct((2, sticks), F32),
            jax.ShapeDtypeStruct((span, 2 * sticks), F32),
        ],
        in_specs=[vmem] * 6,
        out_specs=[vmem] * 2,
        scratch_shapes=[
            pltpu.VMEM((2 * box_edge, sticks), BF16),
            pltpu.VMEM((2, box_edge, grid_len), BF16),
            pltpu.VMEM((4, grid_len // 2, grid_len), F32),
            pltpu.VMEM((2, 2, grid_len // 2, grid_len), BF16),
            pltpu.VMEM((2, grid_len, box_edge), BF16),
            pltpu.VMEM((2 * box_edge, box_edge), BF16),
        ],
        compiler_params=pltpu.CompilerParams(vmem_limit_bytes=16 << 20),
        cost_estimate=pl.CostEstimate(flops=1_400_000_000, bytes_accessed=3 << 20, transcendentals=0),
        name="plane",
    )(planes, *operands)
    backs = pl.pallas_call(
        functools.partial(pair_kernel, mates, count),
        out_shape=jax.ShapeDtypeStruct((mates * groups, 4, stick_dev), F32),
        in_specs=[vmem] * (1 + mates),
        out_specs=vmem,
        scratch_shapes=[pltpu.VMEM((span, 2 * sticks), F32)],
        compiler_params=pltpu.CompilerParams(vmem_limit_bytes=4 << 20),
        name="pairs",
    )(zeds, rows, *others)
    back = lax.all_to_all(
        backs,
        ("band", "pw"),
        split_axis=0,
        concat_axis=0,
        tiled=True,
        axis_index_groups=second,
    )
    applied, correlation = pl.pallas_call(
        functools.partial(tail_kernel, mates, 1.0 / math.sqrt(slab_len * sticks)),
        out_shape=[
            jax.ShapeDtypeStruct((2, stick_dev, box_edge), BF16),
            jax.ShapeDtypeStruct((2, 1, bands), F32),
        ],
        in_specs=[vmem] * 3,
        out_specs=[hbm] * 2,
        scratch_shapes=[
            pltpu.VMEM((2, stick_dev, box_edge), BF16),
            pltpu.VMEM((2, 1, bands), F32),
            pltpu.SemaphoreType.DMA((3,)),
        ],
        compiler_params=pltpu.CompilerParams(vmem_limit_bytes=4 << 20),
        name="tail",
    )(back, columns, z_forward)
    return applied[None], correlation.transpose(0, 2, 1)


def solution(mesh):
    return jax.shard_map(
        local,
        mesh=mesh,
        in_specs=(P("band", None, "pw", None), P("pw", None, None), P()),
        out_specs=(P("band", None, "pw", None), P(None, None, "band")),
        check_vma=False,
    )
```

```python
import functools
import math

import jax
import jax.numpy as jnp
import numpy as np
from jax import lax
from jax.experimental import pallas as pl
from jax.experimental.pallas import tpu as pltpu
from jax.sharding import PartitionSpec as P

F32 = jnp.float32
BF16 = jnp.bfloat16


def first_place(group, groups):
    return ((groups - 3) - group) % groups


def place_of(group, mate, groups, mates):
    return (groups - 1 - group) % groups * mates + mates - 1 - mate


def side_of(mates):
    band = lax.axis_index("band")
    return lax.rem(lax.rem(band, mates) + (mates - 1) * (band // mates), mates)


def lead_pair(side, mates):
    return side % mates


def phases(box_index, grid_index, period, factor):
    turns = box_index[:, None] * grid_index[None, :] % period
    angles = turns * (2.0 * math.pi / period)
    return np.cos(angles) * factor, np.sin(angles) * factor


def plane_tables(box_edge, grid_len):
    half = grid_len // 2
    mats = []
    for parity in range(2):
        cos, sin = phases(
            np.arange(parity, box_edge, 2) - box_edge // 2, np.arange(half), grid_len, 1.0 / math.sqrt(box_edge)
        )
        mats.append(np.block([[cos, sin], [-sin, cos]]))
    mats = np.stack(mats)
    return jnp.asarray(mats[:, : box_edge // 2], BF16), jnp.asarray(mats.transpose(0, 2, 1)[:, :half], BF16)


def z_tables(box_edge, slab_len, grid_len):
    cos, sin = phases(np.arange(box_edge) - box_edge // 2, np.arange(slab_len), grid_len, 1.0)
    inverse = np.stack([np.concatenate([cos.T, -sin.T], 1), np.concatenate([sin.T, cos.T], 1)], 1)
    inverse = inverse.reshape(2 * slab_len, 2 * box_edge) / math.sqrt(box_edge)
    forward = np.block([[cos.T, -sin.T], [sin.T, cos.T]]) / math.sqrt(slab_len)
    return jnp.asarray(inverse, BF16), jnp.asarray(forward, BF16)


def dot_nt(left, right):
    return lax.dot_general(left, right, (((1,), (1,)), ((), ())), preferred_element_type=F32)


def dot_tn(left, right):
    return lax.dot_general(left, right, (((0,), (0,)), ((), ())), preferred_element_type=F32)


def dot_nn(left, right):
    return jnp.dot(left, right, preferred_element_type=F32)


def own_sphere(sticks_ref, stick_dev, box_edge):
    middle = box_edge // 2
    start = pl.multiple_of(lax.axis_index("pw") * stick_dev, stick_dev)
    own = sticks_ref[:, pl.ds(start, stick_dev)] - middle
    own = (own * own).astype(F32)
    radial = own[0:1] + own[1:2]
    column = jnp.broadcast_to(radial, (8, stick_dev)).T[:, 0:1]
    level = lax.broadcasted_iota(jnp.int32, (1, box_edge), 1) - middle
    return column + (level * level).astype(F32) < float(middle * middle)


def head_kernel(
    count,
    coeffs_hbm,
    sticks_hbm,
    table_hbm,
    pot_hbm,
    fwd_hbm,
    tr_hbm,
    out_ref,
    hot_a,
    hot_b,
    pot_ref,
    fwd_ref,
    tr_ref,
    coeffs_ref,
    sticks_ref,
    table_ref,
    sems,
):
    side, n_half = fwd_hbm.shape[1], tr_hbm.shape[1]
    pairs = [
        (sticks_hbm, sticks_ref),
        (table_hbm, table_ref),
        (coeffs_hbm, coeffs_ref),
        (fwd_hbm, fwd_ref.at[:, :side]),
        (tr_hbm, tr_ref.at[:, :n_half]),
        (pot_hbm, pot_ref),
    ]
    copies = [pltpu.make_async_copy(src, dst, sems.at[n]) for n, (src, dst) in enumerate(pairs)]
    for n, copy in enumerate(copies):
        copy.start(priority=int(n not in (0, 2)))
    _, stick_dev, box_edge = coeffs_ref.shape
    slab_len = table_ref.shape[0] // 2
    copies[0].wait()
    sphere = own_sphere(sticks_ref, stick_dev, box_edge)
    copies[2].wait()
    copies[1].wait()
    masked = [jnp.where(sphere, coeffs_ref[c].astype(F32), 0.0).astype(BF16) for c in range(2)]
    masked = jnp.concatenate(masked, axis=1)
    rows = dot_nt(table_ref[...], masked).astype(BF16).astype(F32)
    for z in range(slab_len):
        for t in range(count):
            out_ref[first_place(z, slab_len) * count + t] = rows[2 * z : 2 * z + 2]

    codes = sticks_ref[...]
    codes = ((codes & 1) * side + (codes >> 1)).astype(F32).astype(BF16)
    rows = lax.broadcasted_iota(jnp.int32, (box_edge, stick_dev), 0).astype(F32).astype(BF16)
    one, none = jnp.ones((), BF16), jnp.zeros((), BF16)
    for at in range(0, codes.shape[1], stick_dev):
        cols = slice(at, at + stick_dev)
        hot_a[:, cols] = jnp.where(rows == codes[0:1, cols], one, none)
        hot_b[:, cols] = jnp.where(rows == codes[1:2, cols], one, none)
    for copy in copies[3:5]:
        copy.wait()
    for p in range(2):
        fwd_ref[p, side:, :n_half] = -fwd_ref[p, :side, n_half:]
        fwd_ref[p, side:, n_half:] = fwd_ref[p, :side, :n_half]
        tr_ref[p, n_half:, :side] = -tr_ref[p, :n_half, side:]
        tr_ref[p, n_half:, side:] = tr_ref[p, :n_half, :side]
    copies[5].wait()


def plane_kernel(
    mates,
    count,
    recv_ref,
    hot_a,
    hot_b,
    pot_ref,
    fwd_ref,
    tr_ref,
    back_ref,
    zeds_ref,
    spread,
    half_ref,
    wide_ref,
    left_ref,
    mid_ref,
    cell_ref,
):
    box_edge, sticks = hot_a.shape
    side = box_edge // 2
    groups = recv_ref.shape[0] // count
    per = sticks // groups
    grid_len = pot_ref.shape[0]
    n_half = grid_len // 2

    own_place = lax.rem(lax.axis_index("band") // mates - lead_pair(side_of(mates), mates) + count, count)
    for g in range(groups):
        cols = slice(g * per, (g + 1) * per)
        own = recv_ref[first_place(g, groups) * count + own_place].astype(BF16)
        for c in range(2):
            placed = hot_b[:, cols] * own[c : c + 1]
            for p in range(2):
                row = p * box_edge + c * side
                spread[row : row + side, cols] = placed[p * side : (p + 1) * side]

    box = dot_nt(hot_a[...], spread[...]).astype(BF16)
    for p in range(2):
        wide_ref[p] = dot_nn(box[:, p * box_edge : (p + 1) * box_edge], fwd_ref[p])
    for r in range(0, box_edge, 16):
        even, odd = wide_ref[0, r : r + 16], wide_ref[1, r : r + 16]
        p, at = r // side, r % side
        for n, both in enumerate((even + odd, even - odd)):
            both = both.astype(BF16)
            for c in range(2):
                half_ref[p, c * side + at : c * side + at + 16, n * n_half : (n + 1) * n_half] = both[
                    :, c * n_half : (c + 1) * n_half
                ]

    for c in range(2):
        for p in range(2):
            wide_ref[2 * c + p] = dot_nn(tr_ref[p, c * n_half : (c + 1) * n_half], half_ref[p])
    for r in range(0, n_half, 16):
        rows = slice(r, r + 16)
        pot_near = pot_ref[rows].astype(F32)
        pot_far = pot_ref[n_half + r : n_half + r + 16].astype(F32)
        for c in range(2):
            cols = slice(c * n_half, (c + 1) * n_half)
            even, odd = wide_ref[2 * c, rows], wide_ref[2 * c + 1, rows]
            near = (even + odd) * pot_near
            far = (even - odd) * pot_far
            for p, both in ((0, near + far), (1, near - far)):
                left_ref[p, 0, rows, cols] = (both[:, :n_half] + both[:, n_half:]).astype(BF16)
                left_ref[p, 1, rows, cols] = (both[:, :n_half] - both[:, n_half:]).astype(BF16)
    for p in range(2):
        for q in range(2):
            mid = dot_nt(left_ref[p, q], fwd_ref[q]).astype(BF16)
            for c in range(2):
                mid_ref[p, c * n_half : (c + 1) * n_half, q * side : (q + 1) * side] = mid[
                    :, c * side : (c + 1) * side
                ]

    for p in range(2):
        cell_ref[p * box_edge : (p + 1) * box_edge] = dot_nn(fwd_ref[p], mid_ref[p]).astype(BF16)

    wide = 256
    for s0 in range(0, sticks, wide):
        cols = slice(s0, s0 + wide)
        picked = dot_nn(cell_ref[...], hot_b[:, cols])
        parts = [None, None]
        for p in range(2):
            for r in range(0, side, 16):
                hot = hot_a[p * side + r : p * side + r + 16, cols].astype(F32)
                for c in range(2):
                    at = p * box_edge + c * side + r
                    term = picked[at : at + 16] * hot
                    term = term[:8] + term[8:]
                    parts[c] = term if parts[c] is None else parts[c] + term
        parts = [jnp.sum(part, axis=0, keepdims=True) for part in parts]
        back = jnp.concatenate(parts, axis=0) * (float(box_edge) / float(grid_len))
        back_ref[:, cols] = back.astype(BF16).astype(F32)
    zeds_ref[...] = jnp.zeros_like(zeds_ref)
    gather_rows(count, 0, recv_ref, zeds_ref)


def gather_rows(count, shift, recv_ref, rows_ref):
    groups, per = recv_ref.shape[0] // count, recv_ref.shape[2]
    for t in range(count):
        row = shift * count + t
        for g in range(groups):
            block = recv_ref[first_place(g, groups) * count + t]
            for c in range(2):
                at = (c * groups + g) * per
                rows_ref[row : row + 1, at : at + per] = block[c : c + 1]


def pair_kernel(mates, count, seen_ref, back_ref, *refs):
    others, out_ref, zeds_ref = refs[: mates - 1], refs[mates - 1], refs[mates]
    zeds_ref[...] = seen_ref[...]
    for s in range(1, mates):
        gather_rows(count, s, others[s - 1], zeds_ref)
    back = back_ref[...].astype(BF16)
    left = jnp.concatenate(
        [jnp.concatenate([back[0:1], back[1:2]], axis=1), jnp.concatenate([back[1:2], -back[0:1]], axis=1)], axis=0
    )
    total = dot_nt(left, zeds_ref[...].astype(BF16))
    bands = mates * count
    blocks, _, per = out_ref.shape
    groups = blocks // mates
    for g in range(groups):
        for b in range(mates):
            at = place_of(g, b, groups, mates)
            out_ref[at, 0:2] = back_ref[:, g * per : (g + 1) * per]
            out_ref[at, 2:4, :bands] = total[:, :bands]
            out_ref[at, 2:4, bands:] = jnp.zeros((2, per - bands), F32)


def tail_kernel(mates, scale, recv_ref, sticks_ref, table_ref, out_hbm, corr_hbm, out_ref, corr_ref, sems):
    blocks, _, stick_dev = recv_ref.shape
    groups = blocks // mates
    own_mate = lax.rem(lax.axis_index("band"), mates)
    box_edge = out_ref.shape[2]
    own = [recv_ref[place_of(g, own_mate, groups, mates)] for g in range(groups)]
    total = own[0][2:4]
    for part in own[1:]:
        total = total + part[2:4]
    total = total * scale
    side = side_of(mates)
    count = corr_ref.shape[2] // mates
    for q in range(count):
        for b in range(mates):
            group, at = (b - q) % mates, q * mates + b
            column = None
            for k in range(mates):
                row = (k - group) % mates * count + (q - lead_pair(group, mates)) % count
                here = total[:, row : row + 1]
                column = here if column is None else jnp.where(side == k, here, column)
            for c in range(2):
                corr_ref[c, :, at : at + 1] = column[c : c + 1]
    corr_copy = pltpu.make_async_copy(corr_ref, corr_hbm, sems.at[2])
    corr_copy.start(priority=1)
    sphere = own_sphere(sticks_ref, stick_dev, box_edge)
    back = jnp.concatenate([part[c : c + 1] for c in range(2) for part in own], axis=0).astype(BF16)
    copies = []
    for c in range(2):
        values = dot_tn(back, table_ref[:, c * box_edge : (c + 1) * box_edge])
        out_ref[c] = jnp.where(sphere, values, 0.0).astype(BF16)
        copies.append(pltpu.make_async_copy(out_ref.at[c], out_hbm.at[c], sems.at[c]))
        copies[-1].start(priority=c)
    for copy in copies:
        copy.wait()
    corr_copy.wait()


def local(band_coeffs, potential, stick_list):
    groups = lax.axis_size("pw")
    bands = lax.axis_size("band")
    _, _, stick_dev, box_edge = band_coeffs.shape
    grid_len = potential.shape[1]
    slab_len = potential.shape[0] * groups
    sticks = stick_list.shape[0]
    columns = stick_list.T
    fwd, transposed = plane_tables(box_edge, grid_len)
    z_inverse, z_forward = z_tables(box_edge, slab_len, grid_len)
    in_hbm = functools.partial(pltpu.with_memory_space_constraint, memory_space=pltpu.HBM)
    hbm, vmem = pl.BlockSpec(memory_space=pltpu.HBM), pl.BlockSpec(memory_space=pltpu.VMEM)
    mates = 2 if bands % 2 == 0 else 1
    count = bands // mates

    send, *operands = pl.pallas_call(
        functools.partial(head_kernel, count),
        out_shape=[
            jax.ShapeDtypeStruct((count * groups, 2, stick_dev), F32),
            jax.ShapeDtypeStruct((box_edge, sticks), BF16),
            jax.ShapeDtypeStruct((box_edge, sticks), BF16),
            jax.ShapeDtypeStruct((grid_len, grid_len), BF16),
            jax.ShapeDtypeStruct((2, box_edge, grid_len), BF16),
            jax.ShapeDtypeStruct((2, grid_len, box_edge), BF16),
        ],
        in_specs=[hbm] * 6,
        out_specs=[vmem] * 6,
        scratch_shapes=[
            pltpu.VMEM((2, stick_dev, box_edge), BF16),
            pltpu.VMEM((2, sticks), jnp.int32),
            pltpu.VMEM(z_inverse.shape, BF16),
            pltpu.SemaphoreType.DMA((6,)),
        ],
        compiler_params=pltpu.CompilerParams(vmem_limit_bytes=8 << 20),
        name="head",
    )(
        in_hbm(band_coeffs[0]),
        in_hbm(columns),
        in_hbm(z_inverse),
        in_hbm(potential[0]),
        in_hbm(fwd),
        in_hbm(transposed),
    )
    first = [
        [
            (q * mates + (side + q) % mates) * groups + g
            for g in sorted(range(groups), key=lambda g: first_place(g, groups))
            for q in [(lead_pair(side, mates) + t) % count for t in range(count)]
        ]
        for side in range(mates)
    ]
    second = sorted(
        ((g, b) for g in range(groups) for b in range(mates)), key=lambda member: place_of(*member, groups, mates)
    )
    second = [[(q * mates + b) * groups + g for g, b in second] for q in range(count)]
    planes = lax.all_to_all(
        send, ("band", "pw"), split_axis=0, concat_axis=0, tiled=True, axis_index_groups=first
    )
    others = [
        lax.ppermute(planes, "band", [(b, b - b % mates + (b + s) % mates) for b in range(bands)])
        for s in range(1, mates)
    ]
    span = -(-bands // 8) * 8
    rows, zeds = pl.pallas_call(
        functools.partial(plane_kernel, mates, count),
        out_shape=[
            jax.ShapeDtypeStruct((2, sticks), F32),
            jax.ShapeDtypeStruct((span, 2 * sticks), F32),
        ],
        in_specs=[vmem] * 6,
        out_specs=[vmem] * 2,
        scratch_shapes=[
            pltpu.VMEM((2 * box_edge, sticks), BF16),
            pltpu.VMEM((2, box_edge, grid_len), BF16),
            pltpu.VMEM((4, grid_len // 2, grid_len), F32),
            pltpu.VMEM((2, 2, grid_len // 2, grid_len), BF16),
            pltpu.VMEM((2, grid_len, box_edge), BF16),
            pltpu.VMEM((2 * box_edge, box_edge), BF16),
        ],
        compiler_params=pltpu.CompilerParams(vmem_limit_bytes=16 << 20),
        cost_estimate=pl.CostEstimate(flops=1_400_000_000, bytes_accessed=3 << 20, transcendentals=0),
        name="plane",
    )(planes, *operands)
    backs = pl.pallas_call(
        functools.partial(pair_kernel, mates, count),
        out_shape=jax.ShapeDtypeStruct((mates * groups, 4, stick_dev), F32),
        in_specs=[vmem] * (1 + mates),
        out_specs=vmem,
        scratch_shapes=[pltpu.VMEM((span, 2 * sticks), F32)],
        compiler_params=pltpu.CompilerParams(vmem_limit_bytes=4 << 20),
        name="pairs",
    )(zeds, rows, *others)
    back = lax.all_to_all(
        backs,
        ("band", "pw"),
        split_axis=0,
        concat_axis=0,
        tiled=True,
        axis_index_groups=second,
    )
    applied, correlation = pl.pallas_call(
        functools.partial(tail_kernel, mates, 1.0 / math.sqrt(slab_len * sticks)),
        out_shape=[
            jax.ShapeDtypeStruct((2, stick_dev, box_edge), BF16),
            jax.ShapeDtypeStruct((2, 1, bands), F32),
        ],
        in_specs=[vmem] * 3,
        out_specs=[hbm] * 2,
        scratch_shapes=[
            pltpu.VMEM((2, stick_dev, box_edge), BF16),
            pltpu.VMEM((2, 1, bands), F32),
            pltpu.SemaphoreType.DMA((3,)),
        ],
        compiler_params=pltpu.CompilerParams(vmem_limit_bytes=4 << 20),
        name="tail",
    )(back, columns, z_forward)
    return applied[None], correlation.transpose(0, 2, 1)


def solution(mesh):
    return jax.shard_map(
        local,
        mesh=mesh,
        in_specs=(P("band", None, "pw", None), P("pw", None, None), P()),
        out_specs=(P("band", None, "pw", None), P(None, None, "band")),
        check_vma=False,
    )
```
